256 devices in a mesh: expert: 2 (over core), row: 4 (over x), col: 32 (over z, y).
Axes of the slice: x: 4, y: 4, z: 8, core: 2. Of those that a mesh axis runs over, the one named last changes fastest.
Arguments:
- tokens: bfloat16 [4096, 4096], P(('expert', 'col'), 'row'), may hold values from -6 to 6
- expert_ids: int32 [4096, 2], P(('expert', 'col')), may hold values from 0 to 7, all different within a row; in each aligned block of 64 rows (0 to 63, 64 to 127, ...) at most 20 rows name the same one
- route_weight: float32 [4096, 2], P(('expert', 'col')), may hold values from 0.2 to 1
- gate_projection_weight: bfloat16 [8, 4096, 8192], P('expert', 'row', 'col'), may hold values from -0.09375 to 0.09375
- up_projection_weight: bfloat16 [8, 4096, 8192], P('expert', 'row', 'col'), may hold values from -0.09375 to 0.09375
- down_weight: bfloat16 [8, 8192, 4096], P('expert', 'col', 'row'), may hold values from -0.0625 to 0.0625
Outputs:
- mixed: bfloat16 [4096, 4096], P(('expert', 'col'), 'row')
The draws below stay inside these ranges and needn't reach their ends.
Inputs may be any that keep to these rules, and one draw needn't show every extreme that they name: `expert_ids`: each row names 2 different experts. Among the 64 tokens of one device group (aligned blocks of 64 rows), no expert is named by more than 20 tokens, and in every draw some expert is named by exactly 20 tokens of some block.
All inputs are finite; a program needn't handle non-finite values.
Results may differ from the reference program's by a relative error of at most 0.03.
Values may be sent and summed in bfloat16 or wider, within the bound.
A program may use at most 128 MiB of HBM per device.

```python
import math
import jax
import jax.numpy as jnp
import numpy as np
from jax import lax

D = 4096
FF = 8192
TOP = 2
T_DEV = 64
EXPERTS = 8
TOKENS = 4096
CAP = 20
SLOTS = 1280
N_ROW = 4
N_COL = 32


def shard_levels(own_key, shape, shards, least, largest):
    level = 1.0
    for dim, shards_of in shards:
        steps = jax.random.uniform(jax.random.fold_in(jax.random.fold_in(own_key, 6), dim), (shards_of,), jnp.float32, least / len(shards), largest / len(shards))
        level = level * jnp.repeat(jnp.exp(steps), shape[dim] // shards_of).reshape((-1,) + (1,) * (len(shape) - 1 - dim))
    return level


def assign_block(stream_key, own, number, rows, number_of, top, reach, skew):
    ranking = jax.random.permutation(stream_key, number_of)
    heavy_load, usual = shares(number_of, rows * top, reach, skew, True), shares(number_of, rows * top, reach, skew, False)
    places = jnp.arange(number_of)

    def named(lengths, rotation):
        used = int((lengths > 0).sum())
        fixed = max(1, used // 4)
        moved = fixed + (places - fixed + rotation * (used - fixed)) % max(1, number_of - fixed)
        return jnp.zeros((number_of,), jnp.int32).at[ranking[jnp.where(places < fixed, places, moved)]].set(jnp.asarray(lengths, jnp.int32))

    lengths = jnp.where(number % 4 == 0, named(heavy_load, number // 4), named(usual, number - number // 4 - 1))
    mixed = jax.random.permutation(jax.random.fold_in(own, 3), number_of)
    giver, sink = mixed[0:number_of // 2 * 2:2], mixed[1:number_of // 2 * 2:2]
    margin = jnp.minimum(lengths[giver] - 1, reach - lengths[sink]) // 2
    margin = jnp.where((giver == ranking[0]) | (sink == ranking[0]) | (lengths[sink] == 0), 0, jnp.maximum(margin, 0))
    moved = jax.random.randint(jax.random.fold_in(own, 4), (number_of // 2,), 0, 1 << 20) % (margin + 1)
    lengths = lengths.at[giver].add(-moved).at[sink].add(moved)
    members = jnp.searchsorted(jnp.cumsum(lengths), jnp.arange(rows * top), side="right").astype(jnp.int32)
    listing = members.reshape(top, rows).T
    listing = listing[jax.random.permutation(jax.random.fold_in(own, 1), rows)]
    rotation = jax.random.randint(jax.random.fold_in(own, 2), (rows, 1), 0, top)
    return jnp.take_along_axis(listing, (jnp.arange(top)[None, :] + rotation) % top, axis=1)


def shares(amount, total, limit, skew, full):
    portions = [(1 << 20) // math.isqrt(grade ** skew) + 1 for grade in range(1, amount + 1)]
    largest = limit if full else min(limit, max(-(-total // amount), total * portions[0] // sum(portions)))
    least = 1 if total - largest >= amount - 1 else 0
    given, rest = [largest] + [least] * (amount - 1), total - largest - least * (amount - 1)
    while rest > 0:
        movable = [i for i in range(1, amount) if given[i] < largest] or [i for i in range(1, amount) if given[i] < limit]
        pool, left = sum([portions[i] for i in movable]), rest
        for i in movable:
            more = min(limit - given[i], max(1, left * portions[i] // pool), rest)
            given[i] = given[i] + more
            rest = rest - more
    return np.array(given)


def normal_values(key, extent, spread, bound, cuts=(), kind=jnp.bfloat16):
    level = shard_levels(key, extent, cuts, -0.22, 0.18) if cuts else 1.0
    drawn = jax.random.normal(key, extent, jnp.float32) * spread * level
    return jnp.minimum(jnp.maximum(drawn, -bound), bound).astype(kind)


def setup_inputs(seed: int = 0) -> dict:
    keys = jax.random.split(jax.random.key(seed), 7)
    tokens = normal_values(keys[0], (TOKENS, D), 1.0, 6.0, ((0, 64), (1, 4)))
    expert_ids_keys = jax.random.split(jax.random.fold_in(keys[1], 1), TOKENS // T_DEV)
    expert_ids_turns = jax.random.permutation(jax.random.fold_in(keys[1], 3), TOKENS // T_DEV)
    expert_ids = jax.vmap(lambda own, number: assign_block(jax.random.fold_in(keys[1], 2), own, number, T_DEV, EXPERTS, TOP, CAP, 1))(expert_ids_keys, expert_ids_turns).reshape((TOKENS, TOP))
    route_weight = jnp.clip(0.2 + 0.8 * jax.random.uniform(keys[2], (TOKENS, TOP), jnp.float32) ** shard_levels(keys[2], (TOKENS, TOP), ((0, 64),), -0.2, 0.2), 0.2, 1.0)
    gate_projection_weight = normal_values(keys[3], (EXPERTS, D, FF), D ** -0.5, 0.09375, ((0, 2), (1, 4), (2, 32)))
    up_projection_weight = normal_values(keys[4], (EXPERTS, D, FF), D ** -0.5, 0.09375, ((0, 2), (1, 4), (2, 32)))
    down_weight = normal_values(keys[5], (EXPERTS, FF, D), FF ** -0.5, 0.0625, ((0, 2), (1, 32), (2, 4)))
    return {"tokens": tokens, "expert_ids": expert_ids, "route_weight": route_weight, "gate_projection_weight": gate_projection_weight, "up_projection_weight": up_projection_weight, "down_weight": down_weight}


def round_to_bfloat16(value):
    return lax.optimization_barrier(value.astype(jnp.bfloat16)).astype(jnp.float32)


def blocked_product(left, right, parts):
    row_count, inner = left.shape
    width = inner // parts
    left_blocks = jnp.transpose(left.reshape(row_count, parts, width), (1, 0, 2))
    right_operand_blocks = right.reshape(parts, width, right.shape[1])

    def add_block(running, pair):
        product = jnp.dot(pair[0], pair[1], preferred_element_type=jnp.float32)
        return running + round_to_bfloat16(product), None

    start_value = jnp.zeros((row_count, right.shape[1]), jnp.float32)
    result, _ = lax.scan(add_block, start_value, (left_blocks, right_operand_blocks))
    return result


def reference(tokens, expert_ids, route_weight, gate_projection_weight, up_projection_weight, down_weight):
    slot_total = SLOTS
    token_total = tokens.shape[0]
    tokens_wide = tokens.astype(jnp.float32)

    def one_expert(accum, expert):
        chosen = expert_ids == expert
        picked = jnp.any(chosen, axis=1)
        order = (jnp.cumsum(picked.astype(jnp.int32)) - 1).astype(jnp.int32)
        where_to = jnp.where(picked, order, slot_total).astype(jnp.int32)
        index_list = jnp.zeros((slot_total,), jnp.int32).at[where_to].set(
            jnp.arange(token_total, dtype=jnp.int32), mode="drop")
        rows_per_expert = tokens_wide[index_list]
        gate = blocked_product(rows_per_expert, gate_projection_weight[expert].astype(jnp.float32), N_ROW)
        up = blocked_product(rows_per_expert, up_projection_weight[expert].astype(jnp.float32), N_ROW)
        hidden = round_to_bfloat16(jax.nn.silu(gate) * up)
        expert_out = blocked_product(hidden, down_weight[expert].astype(jnp.float32), N_COL)
        weight_here = jnp.sum(jnp.where(chosen, route_weight, 0.0), axis=1)
        fetched = expert_out[jnp.clip(order, 0, slot_total - 1)]
        contrib = jnp.where(picked[:, None], weight_here[:, None] * fetched, 0.0)
        return accum + contrib, None

    start_value = jnp.zeros((token_total, tokens.shape[1]), jnp.float32)
    mixed, _ = lax.scan(one_expert, start_value, jnp.arange(EXPERTS, dtype=jnp.int32))
    return mixed.astype(jnp.bfloat16)
```

```python
import jax
import jax.numpy as jnp
from jax import lax
from jax.sharding import PartitionSpec as P

SUPER = 256


def on_device(
    tokens, expert_ids, route_weight, gate_projection_weight, up_projection_weight, down_weight
):
    t_dev, feat = tokens.shape
    n_local, _, hid = gate_projection_weight.shape
    n_holders = lax.axis_size("expert")
    n_cols = lax.axis_size("col")
    total = t_dev * n_holders * n_cols
    n_blocks = total // SUPER
    cap = SUPER // t_dev * (5 * t_dev // 16)
    slots = n_local * cap

    everyone = lax.all_gather(lax.all_gather(tokens, "col", tiled=True), "expert", tiled=True)
    ids = lax.all_gather(lax.all_gather(expert_ids, "col", tiled=True), "expert", tiled=True)
    weights = lax.all_gather(lax.all_gather(route_weight, "col", tiled=True), "expert", tiled=True)
    ids = ids.reshape(n_blocks, SUPER, 2)
    weights = weights.reshape(n_blocks, SUPER, 2)

    local = ids - lax.axis_index("expert") * n_local
    names = jnp.arange(n_local, dtype=jnp.int32)
    member = jnp.any(local[..., None] == names, axis=2).astype(jnp.int32)
    rank = jnp.cumsum(member, axis=1) - member
    place = jnp.where(member > 0, rank + names * cap, -1)
    slot = jnp.arange(slots, dtype=jnp.int32)
    hits = place[:, :, :, None] == slot
    table = jnp.any(hits, axis=2)
    share = jnp.sum(
        jnp.where(local[..., None] == names, weights[..., None], 0.0), axis=2
    )
    mix = jnp.sum(jnp.where(hits, share[..., None], 0.0), axis=2)
    slot_weight = jnp.sum(mix, axis=1)
    table = table.astype(jnp.bfloat16)

    rows = jnp.einsum(
        "bts,btd->bsd",
        table,
        everyone.reshape(n_blocks, SUPER, feat),
        preferred_element_type=jnp.float32,
    ).astype(jnp.bfloat16)
    rows = rows.reshape(n_blocks, n_local, cap, feat)
    gate = jnp.einsum(
        "bvsd,vdh->bvsh", rows, gate_projection_weight, preferred_element_type=jnp.float32
    )
    up = jnp.einsum(
        "bvsd,vdh->bvsh", rows, up_projection_weight, preferred_element_type=jnp.float32
    )
    both = jnp.concatenate([gate, up], axis=-1).astype(jnp.bfloat16)
    summed = lax.psum_scatter(both, "row", scatter_dimension=0, tiled=True).astype(jnp.float32)
    hidden = (jax.nn.silu(summed[..., :hid]) * summed[..., hid:]).astype(jnp.bfloat16)
    hidden = lax.all_gather(hidden, "row", axis=0, tiled=True)
    out = jnp.einsum("bvsh,vhd->bvsd", hidden, down_weight, preferred_element_type=jnp.float32)
    out = out.reshape(n_blocks, slots, feat) * slot_weight[..., None]
    mixed = jnp.einsum(
        "bts,bsd->btd", table, out.astype(jnp.bfloat16), preferred_element_type=jnp.float32
    )
    mixed = mixed.astype(jnp.bfloat16).reshape(total, feat)
    mixed = lax.psum_scatter(mixed, "expert", scatter_dimension=0, tiled=True)
    return lax.psum_scatter(mixed, "col", scatter_dimension=0, tiled=True).astype(jnp.bfloat16)


def solution(mesh):
    placed = (
        P(("expert", "col"), "row"),
        P(("expert", "col"), None),
        P(("expert", "col"), None),
        P("expert", "row", "col"),
        P("expert", "row", "col"),
        P("expert", "col", "row"),
    )
    return jax.shard_map(
        on_device,
        mesh=mesh,
        in_specs=placed,
        out_specs=P(("expert", "col"), "row"),
        check_vma=False,
    )
```

```python
import jax
import jax.numpy as jnp
from jax import lax
from jax.experimental import pallas as pl
from jax.experimental.pallas import tpu as pltpu
from jax.sharding import PartitionSpec as P

MESH = pl.DeviceIdType.MESH
BF16 = jnp.bfloat16
F32 = jnp.float32

N_Y = 4
N_Z = 8
N_X = 4
T_DEV = 64
SUPER = N_Y * T_DEV
N_LOCAL = 4
CAP = N_Y * (5 * T_DEV // 16)
SLOTS = N_LOCAL * CAP
ROWS = 2 * CAP
HALF = ROWS // 2
META = 128
ORDER = (0, 1, 3, 4, 5, 7, 6, 2)


def dot(a, b):
    return jnp.dot(a, b, preferred_element_type=F32)


def dot_nt(a, b):
    return lax.dot_general(a, b, (((1,), (1,)), ((), ())), preferred_element_type=F32)


def kernel(
    tok_ref, ids_ref, rw_ref, wg_hbm, wu_hbm, wd_hbm, out_ref,
    wg, wu, wd, tri, eye, xbuf, table, tableT, sw, rowsbuf, gubuf, r1, r2, hbuf, obuf, keep, ces, cer,
    yb, ry1, ry2, zp, zs, zr,
    wsem, ya_s, ya_r, gz_s, gz_r, gx_s, gx_r, x1_s, x1_r, x2_s, x2_r, h_s, h_r, ce_s, ce_r,
    y1_s, y1_r, y2_s, y2_r, z_s, z_r,
):
    feat = tok_ref.shape[1]
    hid = wg.shape[2]
    e = lax.axis_index("expert")
    x = lax.axis_index("row")
    c = lax.axis_index("col")
    z = c // N_Y
    y = c % N_Y
    xp, xm, xo = (x + 1) % N_X, (x + 3) % N_X, (x + 2) % N_X
    yp, ym, yo = (y + 1) % N_Y, (y + 3) % N_Y, (y + 2) % N_Y
    zup, zdn = (z + 1) % N_Z, (z + N_Z - 1) % N_Z
    partner = {"expert": 1 - e}
    dev_xp, dev_xm = {"row": xp}, {"row": xm}
    dev_yp, dev_ym = {"col": z * N_Y + yp}, {"col": z * N_Y + ym}
    dev_zu, dev_zd = {"col": zup * N_Y + y}, {"col": zdn * N_Y + y}

    def send(src, dst, ssem, rsem, dev):
        return pltpu.make_async_remote_copy(
            src_ref=src, dst_ref=dst, send_sem=ssem, recv_sem=rsem, device_id=dev,
            device_id_type=MESH,
        )

    def landed(dst, rsem):
        send(dst, dst, rsem, rsem, partner).wait_recv()

    def left(src, ssem):
        send(src, src, ssem, ssem, partner).wait_send()

    def place(j):
        off = (j // 2) * (1 - j % 2) - ((j + 1) // 2) * (j % 2)
        return (z + off + N_Z) % N_Z

    def arrival(i):
        j = i
        for at, value in enumerate(ORDER):
            j = jnp.where(i == at, value, j)
        return j

    def chunk(i):
        return place(arrival(i))

    weights = [
        pltpu.make_async_copy(wg_hbm, wg, wsem.at[0]),
        pltpu.make_async_copy(wu_hbm, wu, wsem.at[1]),
        pltpu.make_async_copy(wd_hbm, wd, wsem.at[2]),
    ]
    for copy in weights:
        copy.start()

    barrier = pltpu.get_barrier_semaphore()
    for dev in (partner, dev_xp, dev_xm, dev_yp, dev_ym, dev_zu, dev_zd):
        pl.semaphore_signal(barrier, inc=1, device_id=dev, device_id_type=MESH)

    line = lax.broadcasted_iota(jnp.int32, (META, T_DEV), 0)
    lines = jnp.zeros((META, T_DEV), F32)
    for k in range(2):
        lines = jnp.where(line == k, ids_ref[k : k + 1].astype(F32), lines)
        rest = rw_ref[k : k + 1]
        for part in range(3):
            piece = rest.astype(BF16).astype(F32)
            lines = jnp.where(line == 2 + 3 * k + part, piece, lines)
            rest = rest - piece
    same = (
        lax.broadcasted_iota(jnp.int32, (T_DEV, T_DEV), 0)
        == lax.broadcasted_iota(jnp.int32, (T_DEV, T_DEV), 1)
    ).astype(F32).astype(BF16)
    meta = dot_nt(same, lines.astype(BF16))
    own = xbuf.at[z, e, y]
    xbuf[z, e, y, :, 0:feat] = tok_ref[...]
    xbuf[z, e, y, :, feat : feat + META] = meta.astype(BF16)

    across = lax.broadcasted_iota(jnp.int32, (SUPER, SUPER), 0)
    along = lax.broadcasted_iota(jnp.int32, (SUPER, SUPER), 1)
    tri[...] = (across < along).astype(F32).astype(BF16)
    eye[...] = (across == along).astype(F32).astype(BF16)

    pl.semaphore_wait(barrier, 7)

    half = T_DEV // 2
    low, high = pl.ds(0, half), pl.ds(half, half)

    def hop_gz(at):
        j, up = (0, at == 0) if at in (0, 7) else (at, at % 2 == 1)
        part = xbuf.at[place(j), e, y]
        to = j + 2 if j else (1 if up else 2)
        if j > 4:
            part, to = part.at[low if up else high], (7 if up else 8)
        return send(part, part, gz_s.at[at], gz_r.at[to], dev_zu if up else dev_zd)

    def z_pass(j):
        block = xbuf.at[place(j), e, y]
        if j == 7:
            landed(block.at[low], gz_r.at[7])
            landed(block.at[high], gz_r.at[8])
            return
        landed(block, gz_r.at[j])
        hop_gz(j).start()
        landed(xbuf.at[place(j + 1), e, y], gz_r.at[j + 1])
        hop_gz(j + 1).start()

    def hop_ya1(k):
        block = xbuf.at[chunk(k), e, y]
        return (
            send(block, block, ya_s.at[k, 0], ya_r.at[k, 0], dev_yp),
            send(block, block, ya_s.at[k, 1], ya_r.at[k, 1], dev_ym),
        )

    def hop_ya2(k):
        a, b = xbuf.at[chunk(k), e, ym, low], xbuf.at[chunk(k), e, yp, high]
        return (
            send(a, a, ya_s.at[k, 2], ya_r.at[k, 2], dev_yp),
            send(b, b, ya_s.at[k, 3], ya_r.at[k, 3], dev_ym),
        )

    def hop_gx(k):
        block = xbuf.at[chunk(k), e]
        return send(block, block, gx_s.at[k], gx_r.at[k], partner)

    def stage_y1(k):
        for copy in hop_ya1(k):
            copy.start()

    def stage_y2(k):
        to_p, to_m = hop_ya2(k)
        landed(xbuf.at[chunk(k), e, ym], ya_r.at[k, 0])
        to_p.start()
        landed(xbuf.at[chunk(k), e, yp], ya_r.at[k, 1])
        to_m.start()

    def stage_y3(k):
        landed(xbuf.at[chunk(k), e, yo, low], ya_r.at[k, 2])
        landed(xbuf.at[chunk(k), e, yo, high], ya_r.at[k, 3])
        hop_gx(k).start()

    stage_y1(0)
    hop_gz(0).start()
    hop_gz(7).start()
    stage_y2(0)
    z_pass(1)
    stage_y1(1)
    stage_y3(0)
    for copy in weights:
        copy.wait()

    def stage_a1(i):
        zc = chunk(i)
        par = i % 3
        landed(xbuf.at[zc, 1 - e], gx_r.at[i])
        pick = (
            lax.broadcasted_iota(jnp.int32, (16, META), 0)
            == lax.broadcasted_iota(jnp.int32, (16, META), 1)
        ).astype(F32).astype(BF16)
        ex = lax.broadcasted_iota(jnp.int32, (8, SUPER), 0).astype(F32)
        slot = lax.broadcasted_iota(jnp.int32, (CAP, SUPER), 0).astype(F32)
        base = (e * N_LOCAL).astype(F32)
        for s in range(2):
            info = xbuf[zc, s, :, :, feat : feat + META].reshape(SUPER, META)
            rows = dot_nt(pick, info)
            id0 = rows[0:1] - base
            id1 = rows[1:2] - base
            w0 = rows[2:3] + rows[3:4] + rows[4:5]
            w1 = rows[5:6] + rows[6:7] + rows[7:8]
            member = jnp.logical_or(ex == id0, ex == id1).astype(F32)
            rank = dot(member.astype(BF16), tri[...])
            rank = jnp.where(member > 0.5, rank, -1.0)
            for v in range(N_LOCAL):
                hit = (rank[v : v + 1] == slot).astype(F32)
                share = jnp.where(id0 == v, w0, 0.0) + jnp.where(id1 == v, w1, 0.0)
                table[par, s, v * CAP : (v + 1) * CAP, :] = hit.astype(BF16)
                sw[par, v, s * CAP : (s + 1) * CAP, :] = jnp.broadcast_to(
                    jnp.sum(hit * share, axis=1, keepdims=True), (CAP, 128)
                )
            tableT[par, s] = dot_nt(eye[...], table[par, s]).astype(BF16)
            for n in range(0, feat, 256):
                got = dot(
                    table[par, s], xbuf[zc, s, :, :, n : n + 256].reshape(SUPER, 256)
                ).astype(BF16)
                for v in range(N_LOCAL):
                    rowsbuf[v, s * CAP : (s + 1) * CAP, n : n + 256] = got[
                        v * CAP : (v + 1) * CAP
                    ]

    def stage_a2(i):
        par = i % 2

        def up_one(v, carry):
            rows = rowsbuf[v]
            gubuf[par, v, :, 0:hid] = dot(rows, wg[v]).astype(BF16)
            gubuf[par, v, :, hid : 2 * hid] = dot(rows, wu[v]).astype(BF16)
            return carry

        lax.fori_loop(0, N_LOCAL, up_one, 0, unroll=True)
        for copy in hop_x1(i):
            copy.start()

    top, bot = pl.ds(0, HALF), pl.ds(HALF, HALF)

    def hop_x1(i):
        g = gubuf.at[i % 2]
        return (
            send(g.at[xo, top], r1.at[i, 0], x1_s.at[i, 0], x1_r.at[i, 0], dev_xp),
            send(g.at[xo, bot], r1.at[i, 1], x1_s.at[i, 1], x1_r.at[i, 1], dev_xm),
        )

    def hop_x2(i):
        g = gubuf.at[i % 2]
        return (
            send(g.at[xp], r2.at[i, 0], x2_s.at[i, 0], x2_r.at[i, 0], dev_xp),
            send(g.at[xm], r2.at[i, 1], x2_s.at[i, 1], x2_r.at[i, 1], dev_xm),
        )

    def stage_c(i):
        par = i % 2
        to_p, to_m = hop_x2(i)
        landed(r1.at[i, 0], x1_r.at[i, 0])
        gubuf[par, xp, top] = (
            gubuf[par, xp, top].astype(F32) + r1[i, 0].astype(F32)
        ).astype(BF16)
        to_p.start()
        landed(r1.at[i, 1], x1_r.at[i, 1])
        gubuf[par, xm, bot] = (
            gubuf[par, xm, bot].astype(F32) + r1[i, 1].astype(F32)
        ).astype(BF16)
        to_m.start()

    def hop_h1(i):
        mine = hbuf.at[i, x]
        return (
            send(mine, mine, h_s.at[i, 0], h_r.at[i, 0], dev_xp),
            send(mine, mine, h_s.at[i, 1], h_r.at[i, 1], dev_xm),
        )

    def hop_h2(i):
        a, b = hbuf.at[i, xm, top], hbuf.at[i, xp, bot]
        return (
            send(a, a, h_s.at[i, 2], h_r.at[i, 2], dev_xp),
            send(b, b, h_s.at[i, 3], h_r.at[i, 3], dev_xm),
        )

    def stage_b(i):
        par = i % 2
        landed(r2.at[i, 0], x2_r.at[i, 0])
        landed(r2.at[i, 1], x2_r.at[i, 1])
        total = (
            gubuf[par, x].astype(F32) + r2[i, 0].astype(F32) + r2[i, 1].astype(F32)
        )
        gate, up = total[:, 0:hid], total[:, hid : 2 * hid]
        hbuf[i, x] = (gate / (1.0 + jnp.exp(-gate)) * up).astype(BF16)
        for copy in hop_h1(i):
            copy.start()
        for copy in hop_x1(i) + hop_x2(i):
            copy.wait_send()

    def stage_d(i):
        to_p, to_m = hop_h2(i)
        landed(hbuf.at[i, xm], h_r.at[i, 0])
        to_p.start()
        landed(hbuf.at[i, xp], h_r.at[i, 1])
        to_m.start()

    def hop_ce(i):
        return send(ces, cer.at[i], ce_s.at[i], ce_r.at[i], partner)

    def stage_e1(i):
        par = i % 3
        landed(hbuf.at[i, xo, top], h_r.at[i, 2])
        landed(hbuf.at[i, xo, bot], h_r.at[i, 3])

        def down_one(v, carry):
            scale = sw[par, v][:, 0:1]
            for n in range(0, feat, 256):
                res = (dot(hbuf[i, v], wd[v, :, n : n + 256]) * scale).astype(BF16)
                for s in range(2):
                    obuf[s, pl.ds(pl.multiple_of(v * CAP, CAP), CAP), n : n + 256] = res[
                        s * CAP : (s + 1) * CAP
                    ]
            return carry

        lax.fori_loop(0, N_LOCAL, down_one, 0, unroll=True)

    def stage_e2(i):
        par = i % 3
        for n in range(0, feat, 256):
            ces[:, n : n + 256] = dot(
                tableT[par, 1 - e], obuf[1 - e, :, n : n + 256]
            ).astype(BF16)
        hop_ce(i).start()
        for n in range(0, feat, 256):
            keep[:, n : n + 256] = dot(tableT[par, e], obuf[e, :, n : n + 256])
        for copy in hop_h1(i) + hop_h2(i):
            copy.wait_send()

    def hop_y1(i):
        return (
            send(yb.at[yo, low], ry1.at[i, 0], y1_s.at[i, 0], y1_r.at[i, 0], dev_yp),
            send(yb.at[yo, high], ry1.at[i, 1], y1_s.at[i, 1], y1_r.at[i, 1], dev_ym),
            send(yb.at[yp, high], ry2.at[i, 0, high], y1_s.at[i, 2], y1_r.at[i, 2], dev_yp),
            send(yb.at[ym, low], ry2.at[i, 1, low], y1_s.at[i, 3], y1_r.at[i, 3], dev_ym),
        )

    def hop_y2(i):
        return (
            send(yb.at[yp, low], ry2.at[i, 0, low], y2_s.at[i, 0], y2_r.at[i, 0], dev_yp),
            send(yb.at[ym, high], ry2.at[i, 1, high], y2_s.at[i, 1], y2_r.at[i, 1], dev_ym),
        )

    def stage_f(i):
        hop = hop_ce(i)
        hop.wait_recv()
        for b in range(N_Y):
            part = slice(b * T_DEV, (b + 1) * T_DEV)
            yb[b] = (keep[part] + cer[i, part].astype(F32)).astype(BF16)
        for copy in hop_y1(i):
            copy.start()
        hop.wait_send()

    def stage_g(i):
        to_p, to_m = hop_y2(i)
        landed(ry1.at[i, 0], y1_r.at[i, 0])
        yb[yp, low] = (yb[yp, low].astype(F32) + ry1[i, 0].astype(F32)).astype(BF16)
        to_p.start()
        landed(ry1.at[i, 1], y1_r.at[i, 1])
        yb[ym, high] = (yb[ym, high].astype(F32) + ry1[i, 1].astype(F32)).astype(BF16)
        to_m.start()

    def stage_h(i):
        landed(ry2.at[i, 0, high], y1_r.at[i, 2])
        landed(ry2.at[i, 1, low], y1_r.at[i, 3])
        landed(ry2.at[i, 0, low], y2_r.at[i, 0])
        landed(ry2.at[i, 1, high], y2_r.at[i, 1])
        zp[chunk(i)] = yb[y].astype(F32) + ry2[i, 0].astype(F32) + ry2[i, 1].astype(F32)
        for copy in hop_y1(i) + hop_y2(i):
            copy.wait_send()

    def hop_z(k, way):
        dev = dev_zd if way == 0 else dev_zu
        part = zs.at[way, k]
        into = zr.at[way, k]
        if k == 0:
            rows = low if way == 0 else high
            part, into = part.at[rows], into.at[rows]
        return send(part, into, z_s.at[way, k], z_r.at[way, k], dev)

    def stage_z(k, way):
        far = 4 - k
        dest = (z + (N_Z - far if way == 0 else far)) % N_Z
        rows, other = (low, high) if way == 0 else (high, low)
        if k == 0:
            zs[way, k, rows] = zp[dest, rows].astype(BF16)
        elif k == 1:
            landed(zr.at[way, 0, rows], z_r.at[way, 0])
            zs[way, k, other] = zp[dest, other].astype(BF16)
            zs[way, k, rows] = (zp[dest, rows] + zr[way, 0, rows].astype(F32)).astype(BF16)
        else:
            landed(zr.at[way, k - 1], z_r.at[way, k - 1])
            zs[way, k] = (zp[dest] + zr[way, k - 1].astype(F32)).astype(BF16)
        hop_z(k, way).start()

    def body(i, carry):
        def at(lag, *stages):
            @pl.when(jnp.logical_and(i >= lag, i < N_Z + lag))
            def _():
                for stage in stages:
                    stage(i - lag)

        def once(when, stage, *given):
            @pl.when(i == when)
            def _():
                stage(*given)

        at(0, stage_a1)
        at(2, stage_d)
        once(0, stage_y2, 1)
        once(0, z_pass, 3)
        at(0, stage_a2)
        at(-1, stage_y3)
        at(-2, stage_y1)
        at(4, stage_h)
        at(3, stage_f)
        for k in range(3):

            @pl.when(i == N_Z + 1 + k)
            def _(k=k):
                stage_z(k, 0)
                stage_z(k, 1)

        at(2, stage_e1)
        at(1, stage_b)
        at(2, stage_e2)
        at(0, stage_c)
        at(3, stage_g)
        at(-2, stage_y2)
        once(0, z_pass, 5)
        once(1, z_pass, 7)
        return carry

    lax.fori_loop(0, N_Z + 4, body, 0)
    stage_z(3, 0)
    stage_z(3, 1)
    landed(zr.at[0, 3], z_r.at[0, 3])
    landed(zr.at[1, 3], z_r.at[1, 3])
    out_ref[...] = (zp[z] + zr[0, 3].astype(F32) + zr[1, 3].astype(F32)).astype(BF16)
    for k in range(4):
        for way in range(2):
            hop_z(k, way).wait_send()

    for at in range(8):
        hop_gz(at).wait_send()

    def gone(k, carry):
        for copy in hop_ya1(k) + hop_ya2(k):
            copy.wait_send()
        hop_gx(k).wait_send()
        return carry

    lax.fori_loop(0, N_Z, gone, 0)


def on_device(tokens, expert_ids, route_weight, gate_w, up_w, down_w):
    t_dev, feat = tokens.shape
    n_local, _, hid = gate_w.shape
    vmem = pl.BlockSpec(memory_space=pltpu.VMEM)
    hbm = pl.BlockSpec(memory_space=pl.ANY)
    dma = pltpu.SemaphoreType.DMA
    wide = feat + META
    return pl.pallas_call(
        kernel,
        out_shape=jax.ShapeDtypeStruct((t_dev, feat), BF16),
        in_specs=[vmem, vmem, vmem, hbm, hbm, hbm],
        out_specs=vmem,
        scratch_shapes=[
            pltpu.VMEM((n_local, feat, hid), BF16),
            pltpu.VMEM((n_local, feat, hid), BF16),
            pltpu.VMEM((n_local, hid, feat), BF16),
            pltpu.VMEM((SUPER, SUPER), BF16),
            pltpu.VMEM((SUPER, SUPER), BF16),
            pltpu.VMEM((N_Z, 2, N_Y, T_DEV, wide), BF16),
            pltpu.VMEM((3, 2, SLOTS, SUPER), BF16),
            pltpu.VMEM((3, 2, SUPER, SLOTS), BF16),
            pltpu.VMEM((3, N_LOCAL, ROWS, 128), F32),
            pltpu.VMEM((N_LOCAL, ROWS, feat), BF16),
            pltpu.VMEM((2, N_LOCAL, ROWS, 2 * hid), BF16),
            pltpu.VMEM((N_Z, 2, HALF, 2 * hid), BF16),
            pltpu.VMEM((N_Z, 2, ROWS, 2 * hid), BF16),
            pltpu.VMEM((N_Z, N_LOCAL, ROWS, hid), BF16),
            pltpu.VMEM((2, SLOTS, feat), BF16),
            pltpu.VMEM((SUPER, feat), F32),
            pltpu.VMEM((SUPER, feat), BF16),
            pltpu.VMEM((N_Z, SUPER, feat), BF16),
            pltpu.VMEM((N_Y, T_DEV, feat), BF16),
            pltpu.VMEM((N_Z, 2, T_DEV // 2, feat), BF16),
            pltpu.VMEM((N_Z, 2, T_DEV, feat), BF16),
            pltpu.VMEM((N_Z, T_DEV, feat), F32),
            pltpu.VMEM((2, 4, T_DEV, feat), BF16),
            pltpu.VMEM((2, 4, T_DEV, feat), BF16),
            dma((3,)),
            dma((8, 4)), dma((8, 4)),
            dma((8,)), dma((9,)),
            dma((8,)), dma((8,)),
            dma((8, 2)), dma((8, 2)),
            dma((8, 2)), dma((8, 2)),
            dma((8, 4)), dma((8, 4)),
            dma((8,)), dma((8,)),
            dma((8, 4)), dma((8, 4)),
            dma((8, 2)), dma((8, 2)),
            dma((2, 4)), dma((2, 4)),
        ],
        compiler_params=pltpu.CompilerParams(
            collective_id=0, has_side_effects=True, vmem_limit_bytes=58 * 1024 * 1024
        ),
        cost_estimate=pl.CostEstimate(
            flops=12_000_000_000, bytes_accessed=8_000_000, transcendentals=2_000_000
        ),
        name="moe_layer",
    )(tokens, expert_ids.T, route_weight.T, gate_w, up_w, down_w)


def solution(mesh):
    placed = (
        P(("expert", "col"), "row"),
        P(("expert", "col"), None),
        P(("expert", "col"), None),
        P("expert", "row", "col"),
        P("expert", "row", "col"),
        P("expert", "col", "row"),
    )
    return jax.shard_map(
        on_device,
        mesh=mesh,
        in_specs=placed,
        out_specs=P(("expert", "col"), "row"),
        check_vma=False,
    )
```

```python
import jax
import jax.numpy as jnp
from jax import lax
from jax.experimental import pallas as pl
from jax.experimental.pallas import tpu as pltpu
from jax.sharding import PartitionSpec as P

MESH = pl.DeviceIdType.MESH
BF16 = jnp.bfloat16
F32 = jnp.float32

N_Y = 4
N_Z = 8
N_X = 4
T_DEV = 64
SUPER = N_Y * T_DEV
N_LOCAL = 4
CAP = N_Y * (5 * T_DEV // 16)
SLOTS = N_LOCAL * CAP
ROWS = 2 * CAP
HALF = ROWS // 2
META = 128
ORDER = (0, 1, 3, 4, 5, 7, 6, 2)


def dot(a, b):
    return jnp.dot(a, b, preferred_element_type=F32)


def dot_nt(a, b):
    return lax.dot_general(a, b, (((1,), (1,)), ((), ())), preferred_element_type=F32)


def kernel(
    tok_ref, ids_ref, rw_ref, wg_hbm, wu_hbm, wd_hbm, out_ref,
    wg, wu, wd, tri, eye, xbuf, table, tableT, sw, rowsbuf, gubuf, r1, r2, hbuf, obuf, keep, ces, cer,
    yb, ry1, ry2, zp, zs, zr,
    wsem, ya_s, ya_r, gz_s, gz_r, gx_s, gx_r, x_s, x1_r, x2_r, h_s, h1_r, h2_r, ce_s, ce_r,
    y_s, y1_r, y2_r, z_s, z_r,
):
    feat = tok_ref.shape[1]
    hid = wg.shape[2]
    e = lax.axis_index("expert")
    x = lax.axis_index("row")
    c = lax.axis_index("col")
    z = c // N_Y
    y = c % N_Y
    xp, xm, xo = (x + 1) % N_X, (x + 3) % N_X, (x + 2) % N_X
    yp, ym, yo = (y + 1) % N_Y, (y + 3) % N_Y, (y + 2) % N_Y
    zup, zdn = (z + 1) % N_Z, (z + N_Z - 1) % N_Z
    partner = (1 - e, x, c)
    dev_xp, dev_xm = (e, xp, c), (e, xm, c)
    dev_yp, dev_ym = (e, x, z * N_Y + yp), (e, x, z * N_Y + ym)
    dev_zu, dev_zd = (e, x, zup * N_Y + y), (e, x, zdn * N_Y + y)

    def send(src, dst, ssem, rsem, dev):
        return pltpu.make_async_remote_copy(
            src_ref=src, dst_ref=dst, send_sem=ssem, recv_sem=rsem, device_id=dev,
            device_id_type=MESH,
        )

    def landed(dst, rsem):
        send(dst, dst, rsem, rsem, partner).wait_recv()

    def left(src, ssem):
        send(src, src, ssem, ssem, partner).wait_send()

    def place(j):
        off = (j // 2) * (1 - j % 2) - ((j + 1) // 2) * (j % 2)
        return (z + off + N_Z) % N_Z

    def arrival(i):
        j = i
        for at, value in enumerate(ORDER):
            j = jnp.where(i == at, value, j)
        return j

    def chunk(i):
        return place(arrival(i))

    weights = [
        pltpu.make_async_copy(wg_hbm, wg, wsem.at[0]),
        pltpu.make_async_copy(wu_hbm, wu, wsem.at[1]),
        pltpu.make_async_copy(wd_hbm, wd, wsem.at[2]),
    ]
    for copy in weights:
        copy.start()

    barrier = pltpu.get_barrier_semaphore()
    for dev in (partner, dev_xp, dev_xm, dev_yp, dev_ym, dev_zu, dev_zd):
        pl.semaphore_signal(barrier, inc=1, device_id=dev, device_id_type=MESH)

    line = lax.broadcasted_iota(jnp.int32, (META, T_DEV), 0)
    lines = jnp.zeros((META, T_DEV), F32)
    for k in range(2):
        lines = jnp.where(line == k, ids_ref[k : k + 1].astype(F32), lines)
        rest = rw_ref[k : k + 1]
        for part in range(3):
            piece = rest.astype(BF16).astype(F32)
            lines = jnp.where(line == 2 + 3 * k + part, piece, lines)
            rest = rest - piece
    same = (
        lax.broadcasted_iota(jnp.int32, (T_DEV, T_DEV), 0)
        == lax.broadcasted_iota(jnp.int32, (T_DEV, T_DEV), 1)
    ).astype(F32).astype(BF16)
    meta = dot_nt(same, lines.astype(BF16))
    own = xbuf.at[z, e, y]
    xbuf[z, e, y, :, 0:feat] = tok_ref[...]
    xbuf[z, e, y, :, feat : feat + META] = meta.astype(BF16)

    across = lax.broadcasted_iota(jnp.int32, (SUPER, SUPER), 0)
    along = lax.broadcasted_iota(jnp.int32, (SUPER, SUPER), 1)
    tri[...] = (across < along).astype(F32).astype(BF16)
    eye[...] = (across == along).astype(F32).astype(BF16)

    pl.semaphore_wait(barrier, 7)

    def spread(block):
        send(block, block, gz_s.at[0], gz_r.at[1], dev_zu).start()
        send(block, block, gz_s.at[8], gz_r.at[2], dev_zd).start()
        send(block, block, gx_s.at[0], gx_r.at[0], partner).start()

    send(own, own, ya_s.at[0], ya_r.at[0], dev_yp).start()
    send(own, own, ya_s.at[1], ya_r.at[1], dev_ym).start()
    spread(own)
    half = T_DEV // 2
    low, high = pl.ds(0, half), pl.ds(half, half)
    landed(xbuf.at[z, e, ym], ya_r.at[0])
    first = xbuf.at[z, e, ym, low]
    send(first, first, ya_s.at[2], ya_r.at[2], dev_yp).start()
    landed(xbuf.at[z, e, yp], ya_r.at[1])
    second = xbuf.at[z, e, yp, high]
    send(second, second, ya_s.at[3], ya_r.at[3], dev_ym).start()
    spread(xbuf.at[z, e, ym])
    spread(xbuf.at[z, e, yp])
    landed(xbuf.at[z, e, yo, low], ya_r.at[2])
    landed(xbuf.at[z, e, yo, high], ya_r.at[3])
    spread(xbuf.at[z, e, yo])
    left(own, ya_s.at[0])
    left(own, ya_s.at[1])
    left(first, ya_s.at[2])
    left(second, ya_s.at[3])
    for copy in weights:
        copy.wait()

    def pass_on(j):
        down = xbuf.at[place(j), e]
        if j == 7:
            landed(down.at[pl.ds(0, 2)], gz_r.at[7])
            landed(down.at[pl.ds(2, 2)], gz_r.at[8])
            to = ORDER.index(j)
            send(down, down, gx_s.at[to], gx_r.at[to], partner).start()
            return
        upper = xbuf.at[place(j + 1), e]
        landed(down, gz_r.at[j])
        part, to = (down, j + 2) if j < 5 else (down.at[pl.ds(0, 2)], 7)
        send(part, part, gz_s.at[j], gz_r.at[to], dev_zu).start()
        to = ORDER.index(j)
        send(down, down, gx_s.at[to], gx_r.at[to], partner).start()
        landed(upper, gz_r.at[j + 1])
        part, to = (upper, j + 3) if j < 5 else (upper.at[pl.ds(2, 2)], 8)
        send(part, part, gz_s.at[j + 1], gz_r.at[to], dev_zd).start()
        to = ORDER.index(j + 1)
        send(upper, upper, gx_s.at[to], gx_r.at[to], partner).start()

    def stage_a1(i, zc):
        par = lax.rem(i, 3)
        landed(xbuf.at[zc, 1 - e], gx_r.at[i])
        pick = (
            lax.broadcasted_iota(jnp.int32, (16, META), 0)
            == lax.broadcasted_iota(jnp.int32, (16, META), 1)
        ).astype(F32).astype(BF16)
        ex = lax.broadcasted_iota(jnp.int32, (8, SUPER), 0).astype(F32)
        slot = lax.broadcasted_iota(jnp.int32, (CAP, SUPER), 0).astype(F32)
        base = (e * N_LOCAL).astype(F32)
        for s in range(2):
            info = xbuf[zc, s, :, :, feat : feat + META].reshape(SUPER, META)
            rows = dot_nt(pick, info)
            id0 = rows[0:1] - base
            id1 = rows[1:2] - base
            w0 = rows[2:3] + rows[3:4] + rows[4:5]
            w1 = rows[5:6] + rows[6:7] + rows[7:8]
            member = jnp.logical_or(ex == id0, ex == id1).astype(F32)
            rank = dot(member.astype(BF16), tri[...])
            rank = jnp.where(member > 0.5, rank, -1.0)
            for v in range(N_LOCAL):
                hit = (rank[v : v + 1] == slot).astype(F32)
                share = jnp.where(id0 == v, w0, 0.0) + jnp.where(id1 == v, w1, 0.0)
                table[par, s, v * CAP : (v + 1) * CAP, :] = hit.astype(BF16)
                sw[par, v, s * CAP : (s + 1) * CAP, :] = jnp.broadcast_to(
                    jnp.sum(hit * share, axis=1, keepdims=True), (CAP, 128)
                )
            tableT[par, s] = dot_nt(eye[...], table[par, s]).astype(BF16)
            for n in range(0, feat, 256):
                got = dot(
                    table[par, s], xbuf[zc, s, :, :, n : n + 256].reshape(SUPER, 256)
                ).astype(BF16)
                for v in range(N_LOCAL):
                    rowsbuf[v, s * CAP : (s + 1) * CAP, n : n + 256] = got[
                        v * CAP : (v + 1) * CAP
                    ]

    def stage_a2(i):
        par = lax.rem(i, 2)

        def up_one(v, carry):
            rows = rowsbuf[v]
            gubuf[par, v, :, 0:hid] = dot(rows, wg[v]).astype(BF16)
            gubuf[par, v, :, hid : 2 * hid] = dot(rows, wu[v]).astype(BF16)
            return carry

        lax.fori_loop(0, N_LOCAL, up_one, 0, unroll=True)
        for copy in hop_x1(i):
            copy.start()

    top, bot = pl.ds(0, HALF), pl.ds(HALF, HALF)

    def hop_x1(i):
        g = gubuf.at[lax.rem(i, 2)]
        return (
            send(g.at[xo, top], r1.at[i, 0], x_s.at[i], x1_r.at[i], dev_xp),
            send(g.at[xo, bot], r1.at[i, 1], x_s.at[i], x1_r.at[i], dev_xm),
        )

    def hop_x2(i):
        g = gubuf.at[lax.rem(i, 2)]
        return (
            send(g.at[xp], r2.at[i, 0], x_s.at[i], x2_r.at[i], dev_xp),
            send(g.at[xm], r2.at[i, 1], x_s.at[i], x2_r.at[i], dev_xm),
        )

    def stage_c(i):
        par = lax.rem(i, 2)
        to_p, to_m = hop_x2(i)
        landed(r1.at[i], x1_r.at[i])
        gubuf[par, xp, top] = (
            gubuf[par, xp, top].astype(F32) + r1[i, 0].astype(F32)
        ).astype(BF16)
        to_p.start()
        gubuf[par, xm, bot] = (
            gubuf[par, xm, bot].astype(F32) + r1[i, 1].astype(F32)
        ).astype(BF16)
        to_m.start()

    def hop_h1(i):
        mine = hbuf.at[i, x]
        return (
            send(mine, mine, h_s.at[i], h1_r.at[i], dev_xp),
            send(mine, mine, h_s.at[i], h1_r.at[i], dev_xm),
        )

    def hop_h2(i):
        a, b = hbuf.at[i, xm, top], hbuf.at[i, xp, bot]
        return (
            send(a, a, h_s.at[i], h2_r.at[i], dev_xp),
            send(b, b, h_s.at[i], h2_r.at[i], dev_xm),
        )

    def stage_b(i):
        par = lax.rem(i, 2)
        landed(r2.at[i], x2_r.at[i])
        total = (
            gubuf[par, x].astype(F32) + r2[i, 0].astype(F32) + r2[i, 1].astype(F32)
        )
        gate, up = total[:, 0:hid], total[:, hid : 2 * hid]
        hbuf[i, x] = (gate / (1.0 + jnp.exp(-gate)) * up).astype(BF16)
        for copy in hop_h1(i):
            copy.start()
        left(gubuf.at[par, pl.ds(0, 3)], x_s.at[i])

    def stage_d(i):
        to_p, to_m = hop_h2(i)
        landed(hbuf.at[i, pl.ds(0, 2)], h1_r.at[i])
        to_p.start()
        to_m.start()

    def hop_ce(i):
        return send(ces, cer.at[i], ce_s.at[i], ce_r.at[i], partner)

    def stage_e1(i):
        par = lax.rem(i, 3)
        landed(hbuf.at[i, xo], h2_r.at[i])

        def down_one(v, carry):
            scale = jnp.concatenate([sw[par, v], sw[par, v]], axis=1)
            for n in range(0, feat, 256):
                res = (dot(hbuf[i, v], wd[v, :, n : n + 256]) * scale).astype(BF16)
                for s in range(2):
                    obuf[s, pl.ds(pl.multiple_of(v * CAP, CAP), CAP), n : n + 256] = res[
                        s * CAP : (s + 1) * CAP
                    ]
            return carry

        lax.fori_loop(0, N_LOCAL, down_one, 0, unroll=True)

    def stage_e2(i):
        par = lax.rem(i, 3)
        for n in range(0, feat, 256):
            ces[:, n : n + 256] = dot(
                tableT[par, 1 - e], obuf[1 - e, :, n : n + 256]
            ).astype(BF16)
        hop_ce(i).start()
        for n in range(0, feat, 256):
            keep[:, n : n + 256] = dot(tableT[par, e], obuf[e, :, n : n + 256])
        left(hbuf.at[i, pl.ds(0, 3)], h_s.at[i])

    def hop_y1(i):
        return (
            send(yb.at[yo, low], ry1.at[i, 0], y_s.at[i], y1_r.at[i], dev_yp),
            send(yb.at[yo, high], ry1.at[i, 1], y_s.at[i], y1_r.at[i], dev_ym),
        )

    def hop_y2(i):
        return (
            send(yb.at[yp], ry2.at[i, 0], y_s.at[i], y2_r.at[i], dev_yp),
            send(yb.at[ym], ry2.at[i, 1], y_s.at[i], y2_r.at[i], dev_ym),
        )

    def stage_f(i):
        hop = hop_ce(i)
        hop.wait_recv()
        for b in range(N_Y):
            part = slice(b * T_DEV, (b + 1) * T_DEV)
            yb[b] = (keep[part] + cer[i, part].astype(F32)).astype(BF16)
        for copy in hop_y1(i):
            copy.start()
        hop.wait_send()

    def stage_g(i):
        to_p, to_m = hop_y2(i)
        landed(ry1.at[i], y1_r.at[i])
        yb[yp, low] = (yb[yp, low].astype(F32) + ry1[i, 0].astype(F32)).astype(BF16)
        to_p.start()
        yb[ym, high] = (yb[ym, high].astype(F32) + ry1[i, 1].astype(F32)).astype(BF16)
        to_m.start()

    def stage_h(i, zc):
        landed(ry2.at[i], y2_r.at[i])
        zp[zc] = yb[y].astype(F32) + ry2[i, 0].astype(F32) + ry2[i, 1].astype(F32)
        left(yb.at[pl.ds(0, 3)], y_s.at[i])

    def hop_z(k, way):
        dev = dev_zd if way == 0 else dev_zu
        part = zs.at[way, k]
        into = zr.at[way, k]
        if k == 0:
            rows = low if way == 0 else high
            part, into = part.at[rows], into.at[rows]
        return send(part, into, z_s.at[way, k], z_r.at[way, k], dev)

    def stage_z(k, way):
        far = 4 - k
        dest = (z + (N_Z - far if way == 0 else far)) % N_Z
        rows, other = (low, high) if way == 0 else (high, low)
        if k == 0:
            zs[way, k, rows] = zp[dest, rows].astype(BF16)
        elif k == 1:
            landed(zr.at[way, 0, rows], z_r.at[way, 0])
            zs[way, k, other] = zp[dest, other].astype(BF16)
            zs[way, k, rows] = (zp[dest, rows] + zr[way, 0, rows].astype(F32)).astype(BF16)
        else:
            landed(zr.at[way, k - 1], z_r.at[way, k - 1])
            zs[way, k] = (zp[dest] + zr[way, k - 1].astype(F32)).astype(BF16)
        hop_z(k, way).start()

    def body(i, zcs):
        def at(lag, stage, *given):
            @pl.when(jnp.logical_and(i >= lag, i < N_Z + lag))
            def _():
                stage(i - lag, *given)

        at(0, stage_a1, zcs[0])
        at(2, stage_d)
        at(0, stage_a2)
        at(4, stage_h, zcs[4])
        at(3, stage_f)
        for k in range(3):

            @pl.when(i == N_Z + 1 + k)
            def _(k=k):
                stage_z(k, 0)
                stage_z(k, 1)

        at(2, stage_e1)
        at(1, stage_b)
        at(2, stage_e2)
        at(0, stage_c)
        at(3, stage_g)
        for when, j in ((0, 1), (1, 3), (3, 5), (4, 7)):

            @pl.when(i == when)
            def _(j=j):
                pass_on(j)

        return (chunk(i + 1),) + zcs[:4]

    lax.fori_loop(0, N_Z + 4, body, (z,) * 5)
    stage_z(3, 0)
    stage_z(3, 1)
    landed(zr.at[0, 3], z_r.at[0, 3])
    landed(zr.at[1, 3], z_r.at[1, 3])
    out_ref[...] = (zp[z] + zr[0, 3].astype(F32) + zr[1, 3].astype(F32)).astype(BF16)
    for k in range(4):
        for way in range(2):
            hop_z(k, way).wait_send()

    whole = xbuf.at[z, e]
    left(whole, gz_s.at[0])
    left(whole, gz_s.at[8])
    left(whole, gx_s.at[0])
    for j in range(1, 8):
        left(whole, gx_s.at[j])
        if j < 5:
            left(whole, gz_s.at[j])
        elif j < 7:
            left(xbuf.at[z, e, pl.ds(0, 2)], gz_s.at[j])


def on_device(tokens, expert_ids, route_weight, gate_w, up_w, down_w):
    t_dev, feat = tokens.shape
    n_local, _, hid = gate_w.shape
    vmem = pl.BlockSpec(memory_space=pltpu.VMEM)
    hbm = pl.BlockSpec(memory_space=pl.ANY)
    dma = pltpu.SemaphoreType.DMA
    wide = feat + META
    return pl.pallas_call(
        kernel,
        out_shape=jax.ShapeDtypeStruct((t_dev, feat), BF16),
        in_specs=[vmem, vmem, vmem, hbm, hbm, hbm],
        out_specs=vmem,
        scratch_shapes=[
            pltpu.VMEM((n_local, feat, hid), BF16),
            pltpu.VMEM((n_local, feat, hid), BF16),
            pltpu.VMEM((n_local, hid, feat), BF16),
            pltpu.VMEM((SUPER, SUPER), BF16),
            pltpu.VMEM((SUPER, SUPER), BF16),
            pltpu.VMEM((N_Z, 2, N_Y, T_DEV, wide), BF16),
            pltpu.VMEM((3, 2, SLOTS, SUPER), BF16),
            pltpu.VMEM((3, 2, SUPER, SLOTS), BF16),
            pltpu.VMEM((3, N_LOCAL, ROWS, 128), F32),
            pltpu.VMEM((N_LOCAL, ROWS, feat), BF16),
            pltpu.VMEM((2, N_LOCAL, ROWS, 2 * hid), BF16),
            pltpu.VMEM((N_Z, 2, HALF, 2 * hid), BF16),
            pltpu.VMEM((N_Z, 2, ROWS, 2 * hid), BF16),
            pltpu.VMEM((N_Z, N_LOCAL, ROWS, hid), BF16),
            pltpu.VMEM((2, SLOTS, feat), BF16),
            pltpu.VMEM((SUPER, feat), F32),
            pltpu.VMEM((SUPER, feat), BF16),
            pltpu.VMEM((N_Z, SUPER, feat), BF16),
            pltpu.VMEM((N_Y, T_DEV, feat), BF16),
            pltpu.VMEM((N_Z, 2, T_DEV // 2, feat), BF16),
            pltpu.VMEM((N_Z, 2, T_DEV, feat), BF16),
            pltpu.VMEM((N_Z, T_DEV, feat), F32),
            pltpu.VMEM((2, 4, T_DEV, feat), BF16),
            pltpu.VMEM((2, 4, T_DEV, feat), BF16),
            dma((3,)),
            dma((4,)), dma((4,)),
            dma((9,)), dma((9,)),
            dma((8,)), dma((8,)),
            dma((8,)), dma((8,)), dma((8,)),
            dma((8,)), dma((8,)), dma((8,)),
            dma((8,)), dma((8,)),
            dma((8,)), dma((8,)), dma((8,)),
            dma((2, 4)), dma((2, 4)),
        ],
        compiler_params=pltpu.CompilerParams(
            collective_id=0, has_side_effects=True, vmem_limit_bytes=58 * 1024 * 1024
        ),
        cost_estimate=pl.CostEstimate(
            flops=12_000_000_000, bytes_accessed=8_000_000, transcendentals=2_000_000
        ),
        name="moe_layer",
    )(tokens, expert_ids.T, route_weight.T, gate_w, up_w, down_w)


def solution(mesh):
    placed = (
        P(("expert", "col"), "row"),
        P(("expert", "col"), None),
        P(("expert", "col"), None),
        P("expert", "row", "col"),
        P("expert", "row", "col"),
        P("expert", "col", "row"),
    )
    return jax.shard_map(
        on_device,
        mesh=mesh,
        in_specs=placed,
        out_specs=P(("expert", "col"), "row"),
        check_vma=False,
    )
```

```python
import jax
import jax.numpy as jnp
from jax import lax
from jax.experimental import pallas as pl
from jax.experimental.pallas import tpu as pltpu
from jax.sharding import PartitionSpec as P

MESH = pl.DeviceIdType.MESH
BF16 = jnp.bfloat16
F32 = jnp.float32

N_Y = 4
N_Z = 8
N_X = 4
T_DEV = 64
SUPER = N_Y * T_DEV
N_LOCAL = 4
CAP = N_Y * (5 * T_DEV // 16)
SLOTS = N_LOCAL * CAP
ROWS = 2 * CAP
HALF = ROWS // 2
META = 128
ORDER = (0, 1, 3, 4, 5, 7, 6, 2)


def dot(a, b):
    return jnp.dot(a, b, preferred_element_type=F32)


def dot_nt(a, b):
    return lax.dot_general(a, b, (((1,), (1,)), ((), ())), preferred_element_type=F32)


def kernel(
    tok_ref, ids_ref, rw_ref, wg_hbm, wu_hbm, wd_hbm, out_ref,
    wg, wu, wd, tri, eye, xbuf, table, tableT, sw, rowsbuf, gubuf, r1, r2, hbuf, obuf, keep, ces, cer,
    yb, ry1, ry2, zp, zs, zr,
    wsem, ya_s, ya_r, gz_s, gz_r, gx_s, gx_r, x_s, x1_r, x2_r, h_s, h1_r, h2_r, ce_s, ce_r,
    y_s, y1_r, y2_r, z_s, z_r,
):
    feat = tok_ref.shape[1]
    hid = wg.shape[2]
    e = lax.axis_index("expert")
    x = lax.axis_index("row")
    c = lax.axis_index("col")
    z = c // N_Y
    y = c % N_Y
    xp, xm, xo = (x + 1) % N_X, (x + 3) % N_X, (x + 2) % N_X
    yp, ym, yo = (y + 1) % N_Y, (y + 3) % N_Y, (y + 2) % N_Y
    zup, zdn = (z + 1) % N_Z, (z + N_Z - 1) % N_Z
    partner = (1 - e, x, c)
    dev_xp, dev_xm = (e, xp, c), (e, xm, c)
    dev_yp, dev_ym = (e, x, z * N_Y + yp), (e, x, z * N_Y + ym)
    dev_zu, dev_zd = (e, x, zup * N_Y + y), (e, x, zdn * N_Y + y)

    def send(src, dst, ssem, rsem, dev):
        return pltpu.make_async_remote_copy(
            src_ref=src, dst_ref=dst, send_sem=ssem, recv_sem=rsem, device_id=dev,
            device_id_type=MESH,
        )

    def landed(dst, rsem):
        send(dst, dst, rsem, rsem, partner).wait_recv()

    def left(src, ssem):
        send(src, src, ssem, ssem, partner).wait_send()

    def place(j):
        off = (j // 2) * (1 - j % 2) - ((j + 1) // 2) * (j % 2)
        return (z + off + N_Z) % N_Z

    def arrival(i):
        j = i
        for at, value in enumerate(ORDER):
            j = jnp.where(i == at, value, j)
        return j

    def chunk(i):
        return place(arrival(i))

    weights = [
        pltpu.make_async_copy(wg_hbm, wg, wsem.at[0]),
        pltpu.make_async_copy(wu_hbm, wu, wsem.at[1]),
        pltpu.make_async_copy(wd_hbm, wd, wsem.at[2]),
    ]
    for copy in weights:
        copy.start()

    barrier = pltpu.get_barrier_semaphore()
    for dev in (partner, dev_xp, dev_xm, dev_yp, dev_ym, dev_zu, dev_zd):
        pl.semaphore_signal(barrier, inc=1, device_id=dev, device_id_type=MESH)

    line = lax.broadcasted_iota(jnp.int32, (META, T_DEV), 0)
    lines = jnp.zeros((META, T_DEV), F32)
    for k in range(2):
        lines = jnp.where(line == k, ids_ref[k : k + 1].astype(F32), lines)
        rest = rw_ref[k : k + 1]
        for part in range(3):
            piece = rest.astype(BF16).astype(F32)
            lines = jnp.where(line == 2 + 3 * k + part, piece, lines)
            rest = rest - piece
    same = (
        lax.broadcasted_iota(jnp.int32, (T_DEV, T_DEV), 0)
        == lax.broadcasted_iota(jnp.int32, (T_DEV, T_DEV), 1)
    ).astype(F32).astype(BF16)
    meta = dot_nt(same, lines.astype(BF16))
    own = xbuf.at[z, e, y]
    xbuf[z, e, y, :, 0:feat] = tok_ref[...]
    xbuf[z, e, y, :, feat : feat + META] = meta.astype(BF16)

    across = lax.broadcasted_iota(jnp.int32, (SUPER, SUPER), 0)
    along = lax.broadcasted_iota(jnp.int32, (SUPER, SUPER), 1)
    tri[...] = (across < along).astype(F32).astype(BF16)
    eye[...] = (across == along).astype(F32).astype(BF16)

    pl.semaphore_wait(barrier, 7)

    def spread(block):
        send(block, block, gz_s.at[0], gz_r.at[1], dev_zu).start()
        send(block, block, gz_s.at[8], gz_r.at[2], dev_zd).start()
        send(block, block, gx_s.at[0], gx_r.at[0], partner).start()

    send(own, own, ya_s.at[0], ya_r.at[0], dev_yp).start()
    send(own, own, ya_s.at[1], ya_r.at[1], dev_ym).start()
    spread(own)
    half = T_DEV // 2
    low, high = pl.ds(0, half), pl.ds(half, half)
    landed(xbuf.at[z, e, ym], ya_r.at[0])
    first = xbuf.at[z, e, ym, low]
    send(first, first, ya_s.at[2], ya_r.at[2], dev_yp).start()
    landed(xbuf.at[z, e, yp], ya_r.at[1])
    second = xbuf.at[z, e, yp, high]
    send(second, second, ya_s.at[3], ya_r.at[3], dev_ym).start()
    spread(xbuf.at[z, e, ym])
    spread(xbuf.at[z, e, yp])
    landed(xbuf.at[z, e, yo, low], ya_r.at[2])
    landed(xbuf.at[z, e, yo, high], ya_r.at[3])
    spread(xbuf.at[z, e, yo])
    left(own, ya_s.at[0])
    left(own, ya_s.at[1])
    left(first, ya_s.at[2])
    left(second, ya_s.at[3])
    for copy in weights:
        copy.wait()

    def pass_on(j):
        down = xbuf.at[place(j), e]
        if j == 7:
            landed(down.at[pl.ds(0, 2)], gz_r.at[7])
            landed(down.at[pl.ds(2, 2)], gz_r.at[8])
            to = ORDER.index(j)
            send(down, down, gx_s.at[to], gx_r.at[to], partner).start()
            return
        upper = xbuf.at[place(j + 1), e]
        landed(down, gz_r.at[j])
        part, to = (down, j + 2) if j < 5 else (down.at[pl.ds(0, 2)], 7)
        send(part, part, gz_s.at[j], gz_r.at[to], dev_zu).start()
        to = ORDER.index(j)
        send(down, down, gx_s.at[to], gx_r.at[to], partner).start()
        landed(upper, gz_r.at[j + 1])
        part, to = (upper, j + 3) if j < 5 else (upper.at[pl.ds(2, 2)], 8)
        send(part, part, gz_s.at[j + 1], gz_r.at[to], dev_zd).start()
        to = ORDER.index(j + 1)
        send(upper, upper, gx_s.at[to], gx_r.at[to], partner).start()

    def stage_a1(i, zc):
        par = lax.rem(i, 4)
        landed(xbuf.at[zc, 1 - e], gx_r.at[i])
        pick = (
            lax.broadcasted_iota(jnp.int32, (16, META), 0)
            == lax.broadcasted_iota(jnp.int32, (16, META), 1)
        ).astype(F32).astype(BF16)
        ex = lax.broadcasted_iota(jnp.int32, (8, SUPER), 0).astype(F32)
        slot = lax.broadcasted_iota(jnp.int32, (CAP, SUPER), 0).astype(F32)
        base = (e * N_LOCAL).astype(F32)
        for s in range(2):
            info = xbuf[zc, s, :, :, feat : feat + META].reshape(SUPER, META)
            rows = dot_nt(pick, info)
            id0 = rows[0:1] - base
            id1 = rows[1:2] - base
            w0 = rows[2:3] + rows[3:4] + rows[4:5]
            w1 = rows[5:6] + rows[6:7] + rows[7:8]
            member = jnp.logical_or(ex == id0, ex == id1).astype(F32)
            rank = dot(member.astype(BF16), tri[...])
            rank = jnp.where(member > 0.5, rank, -1.0)
            for v in range(N_LOCAL):
                hit = (rank[v : v + 1] == slot).astype(F32)
                share = jnp.where(id0 == v, w0, 0.0) + jnp.where(id1 == v, w1, 0.0)
                table[par, s, v * CAP : (v + 1) * CAP, :] = hit.astype(BF16)
                sw[par, v, s * CAP : (s + 1) * CAP, :] = jnp.broadcast_to(
                    jnp.sum(hit * share, axis=1, keepdims=True), (CAP, 128)
                )
            tableT[par, s] = dot_nt(eye[...], table[par, s]).astype(BF16)
            for n in range(0, feat, 256):
                got = dot(
                    table[par, s], xbuf[zc, s, :, :, n : n + 256].reshape(SUPER, 256)
                ).astype(BF16)
                for v in range(N_LOCAL):
                    rowsbuf[v, s * CAP : (s + 1) * CAP, n : n + 256] = got[
                        v * CAP : (v + 1) * CAP
                    ]

    def stage_a2(i):
        par = lax.rem(i, 3)

        def up_one(v, carry):
            rows = rowsbuf[v]
            gubuf[par, v, :, 0:hid] = dot(rows, wg[v]).astype(BF16)
            gubuf[par, v, :, hid : 2 * hid] = dot(rows, wu[v]).astype(BF16)
            return carry

        lax.fori_loop(0, N_LOCAL, up_one, 0, unroll=True)
        for copy in hop_x1(i):
            copy.start()

    top, bot = pl.ds(0, HALF), pl.ds(HALF, HALF)

    def hop_x1(i):
        g = gubuf.at[lax.rem(i, 3)]
        return (
            send(g.at[xo, top], r1.at[i, 0], x_s.at[i], x1_r.at[i], dev_xp),
            send(g.at[xo, bot], r1.at[i, 1], x_s.at[i], x1_r.at[i], dev_xm),
        )

    def hop_x2(i):
        g = gubuf.at[lax.rem(i, 3)]
        return (
            send(g.at[xp], r2.at[i, 0], x_s.at[i], x2_r.at[i], dev_xp),
            send(g.at[xm], r2.at[i, 1], x_s.at[i], x2_r.at[i], dev_xm),
        )

    def stage_c(i):
        par = lax.rem(i, 3)
        to_p, to_m = hop_x2(i)
        landed(r1.at[i], x1_r.at[i])
        gubuf[par, xp, top] = (
            gubuf[par, xp, top].astype(F32) + r1[i, 0].astype(F32)
        ).astype(BF16)
        to_p.start()
        gubuf[par, xm, bot] = (
            gubuf[par, xm, bot].astype(F32) + r1[i, 1].astype(F32)
        ).astype(BF16)
        to_m.start()

    def hop_h1(i):
        mine = hbuf.at[i, x]
        return (
            send(mine, mine, h_s.at[i], h1_r.at[i], dev_xp),
            send(mine, mine, h_s.at[i], h1_r.at[i], dev_xm),
        )

    def hop_h2(i):
        a, b = hbuf.at[i, xm, top], hbuf.at[i, xp, bot]
        return (
            send(a, a, h_s.at[i], h2_r.at[i], dev_xp),
            send(b, b, h_s.at[i], h2_r.at[i], dev_xm),
        )

    def stage_b(i):
        par = lax.rem(i, 3)
        landed(r2.at[i], x2_r.at[i])
        total = (
            gubuf[par, x].astype(F32) + r2[i, 0].astype(F32) + r2[i, 1].astype(F32)
        )
        gate, up = total[:, 0:hid], total[:, hid : 2 * hid]
        hbuf[i, x] = (gate / (1.0 + jnp.exp(-gate)) * up).astype(BF16)
        for copy in hop_h1(i):
            copy.start()
        left(gubuf.at[par, pl.ds(0, 3)], x_s.at[i])

    def stage_d(i):
        to_p, to_m = hop_h2(i)
        landed(hbuf.at[i, pl.ds(0, 2)], h1_r.at[i])
        to_p.start()
        to_m.start()

    def hop_ce(i):
        return send(ces, cer.at[i], ce_s.at[i], ce_r.at[i], partner)

    def stage_e1(i):
        par = lax.rem(i, 4)
        landed(hbuf.at[i, xo], h2_r.at[i])

        def down_one(v, carry):
            scale = jnp.concatenate([sw[par, v], sw[par, v]], axis=1)
            for n in range(0, feat, 256):
                res = (dot(hbuf[i, v], wd[v, :, n : n + 256]) * scale).astype(BF16)
                for s in range(2):
                    obuf[s, pl.ds(pl.multiple_of(v * CAP, CAP), CAP), n : n + 256] = res[
                        s * CAP : (s + 1) * CAP
                    ]
            return carry

        lax.fori_loop(0, N_LOCAL, down_one, 0, unroll=True)

    def stage_e2(i):
        par = lax.rem(i, 4)
        for n in range(0, feat, 256):
            ces[:, n : n + 256] = dot(
                tableT[par, 1 - e], obuf[1 - e, :, n : n + 256]
            ).astype(BF16)
        hop_ce(i).start()
        for n in range(0, feat, 256):
            keep[:, n : n + 256] = dot(tableT[par, e], obuf[e, :, n : n + 256])
        left(hbuf.at[i, pl.ds(0, 3)], h_s.at[i])

    def hop_y1(i):
        return (
            send(yb.at[yo, low], ry1.at[i, 0], y_s.at[i], y1_r.at[i], dev_yp),
            send(yb.at[yo, high], ry1.at[i, 1], y_s.at[i], y1_r.at[i], dev_ym),
        )

    def hop_y2(i):
        return (
            send(yb.at[yp], ry2.at[i, 0], y_s.at[i], y2_r.at[i], dev_yp),
            send(yb.at[ym], ry2.at[i, 1], y_s.at[i], y2_r.at[i], dev_ym),
        )

    def stage_f(i):
        hop = hop_ce(i)
        hop.wait_recv()
        for b in range(N_Y):
            part = slice(b * T_DEV, (b + 1) * T_DEV)
            yb[b] = (keep[part] + cer[i, part].astype(F32)).astype(BF16)
        for copy in hop_y1(i):
            copy.start()
        hop.wait_send()

    def stage_g(i):
        to_p, to_m = hop_y2(i)
        landed(ry1.at[i], y1_r.at[i])
        yb[yp, low] = (yb[yp, low].astype(F32) + ry1[i, 0].astype(F32)).astype(BF16)
        to_p.start()
        yb[ym, high] = (yb[ym, high].astype(F32) + ry1[i, 1].astype(F32)).astype(BF16)
        to_m.start()

    def stage_h(i, zc):
        landed(ry2.at[i], y2_r.at[i])
        zp[zc] = yb[y].astype(F32) + ry2[i, 0].astype(F32) + ry2[i, 1].astype(F32)
        left(yb.at[pl.ds(0, 3)], y_s.at[i])

    def hop_z(k, way):
        dev = dev_zd if way == 0 else dev_zu
        part = zs.at[way, k]
        into = zr.at[way, k]
        if k == 0:
            rows = low if way == 0 else high
            part, into = part.at[rows], into.at[rows]
        return send(part, into, z_s.at[way, k], z_r.at[way, k], dev)

    def stage_z(k, way):
        far = 4 - k
        dest = (z + (N_Z - far if way == 0 else far)) % N_Z
        rows, other = (low, high) if way == 0 else (high, low)
        if k == 0:
            zs[way, k, rows] = zp[dest, rows].astype(BF16)
        elif k == 1:
            landed(zr.at[way, 0, rows], z_r.at[way, 0])
            zs[way, k, other] = zp[dest, other].astype(BF16)
            zs[way, k, rows] = (zp[dest, rows] + zr[way, 0, rows].astype(F32)).astype(BF16)
        else:
            landed(zr.at[way, k - 1], z_r.at[way, k - 1])
            zs[way, k] = (zp[dest] + zr[way, k - 1].astype(F32)).astype(BF16)
        hop_z(k, way).start()

    def body(i, zcs):
        def at(lag, stage, *given):
            @pl.when(jnp.logical_and(i >= lag, i < N_Z + lag))
            def _():
                stage(i - lag, *given)

        at(0, stage_a1, zcs[0])
        at(0, stage_a2)
        at(1, stage_c)
        at(2, stage_b)
        at(5, stage_h, zcs[5])
        at(4, stage_f)
        for k in range(3):

            @pl.when(i == N_Z + 2 + k)
            def _(k=k):
                stage_z(k, 0)
                stage_z(k, 1)

        at(3, stage_e1)
        at(3, stage_e2)
        at(2, stage_d)
        at(4, stage_g)
        for when, j in ((0, 1), (1, 3), (3, 5), (4, 7)):

            @pl.when(i == when)
            def _(j=j):
                pass_on(j)

        return (chunk(i + 1),) + zcs[:5]

    lax.fori_loop(0, N_Z + 5, body, (z,) * 6)
    stage_z(3, 0)
    stage_z(3, 1)
    landed(zr.at[0, 3], z_r.at[0, 3])
    landed(zr.at[1, 3], z_r.at[1, 3])
    out_ref[...] = (zp[z] + zr[0, 3].astype(F32) + zr[1, 3].astype(F32)).astype(BF16)
    for k in range(4):
        for way in range(2):
            hop_z(k, way).wait_send()

    whole = xbuf.at[z, e]
    left(whole, gz_s.at[0])
    left(whole, gz_s.at[8])
    left(whole, gx_s.at[0])
    for j in range(1, 8):
        left(whole, gx_s.at[j])
        if j < 5:
            left(whole, gz_s.at[j])
        elif j < 7:
            left(xbuf.at[z, e, pl.ds(0, 2)], gz_s.at[j])


def on_device(tokens, expert_ids, route_weight, gate_w, up_w, down_w):
    t_dev, feat = tokens.shape
    n_local, _, hid = gate_w.shape
    vmem = pl.BlockSpec(memory_space=pltpu.VMEM)
    hbm = pl.BlockSpec(memory_space=pl.ANY)
    dma = pltpu.SemaphoreType.DMA
    wide = feat + META
    return pl.pallas_call(
        kernel,
        out_shape=jax.ShapeDtypeStruct((t_dev, feat), BF16),
        in_specs=[vmem, vmem, vmem, hbm, hbm, hbm],
        out_specs=vmem,
        scratch_shapes=[
            pltpu.VMEM((n_local, feat, hid), BF16),
            pltpu.VMEM((n_local, feat, hid), BF16),
            pltpu.VMEM((n_local, hid, feat), BF16),
            pltpu.VMEM((SUPER, SUPER), BF16),
            pltpu.VMEM((SUPER, SUPER), BF16),
            pltpu.VMEM((N_Z, 2, N_Y, T_DEV, wide), BF16),
            pltpu.VMEM((4, 2, SLOTS, SUPER), BF16),
            pltpu.VMEM((4, 2, SUPER, SLOTS), BF16),
            pltpu.VMEM((4, N_LOCAL, ROWS, 128), F32),
            pltpu.VMEM((N_LOCAL, ROWS, feat), BF16),
            pltpu.VMEM((3, N_LOCAL, ROWS, 2 * hid), BF16),
            pltpu.VMEM((N_Z, 2, HALF, 2 * hid), BF16),
            pltpu.VMEM((N_Z, 2, ROWS, 2 * hid), BF16),
            pltpu.VMEM((N_Z, N_LOCAL, ROWS, hid), BF16),
            pltpu.VMEM((2, SLOTS, feat), BF16),
            pltpu.VMEM((SUPER, feat), F32),
            pltpu.VMEM((SUPER, feat), BF16),
            pltpu.VMEM((N_Z, SUPER, feat), BF16),
            pltpu.VMEM((N_Y, T_DEV, feat), BF16),
            pltpu.VMEM((N_Z, 2, T_DEV // 2, feat), BF16),
            pltpu.VMEM((N_Z, 2, T_DEV, feat), BF16),
            pltpu.VMEM((N_Z, T_DEV, feat), F32),
            pltpu.VMEM((2, 4, T_DEV, feat), BF16),
            pltpu.VMEM((2, 4, T_DEV, feat), BF16),
            dma((3,)),
            dma((4,)), dma((4,)),
            dma((9,)), dma((9,)),
            dma((8,)), dma((8,)),
            dma((8,)), dma((8,)), dma((8,)),
            dma((8,)), dma((8,)), dma((8,)),
            dma((8,)), dma((8,)),
            dma((8,)), dma((8,)), dma((8,)),
            dma((2, 4)), dma((2, 4)),
        ],
        compiler_params=pltpu.CompilerParams(
            collective_id=0, has_side_effects=True, vmem_limit_bytes=58 * 1024 * 1024
        ),
        cost_estimate=pl.CostEstimate(
            flops=12_000_000_000, bytes_accessed=8_000_000, transcendentals=2_000_000
        ),
        name="moe_layer",
    )(tokens, expert_ids.T, route_weight.T, gate_w, up_w, down_w)


def solution(mesh):
    placed = (
        P(("expert", "col"), "row"),
        P(("expert", "col"), None),
        P(("expert", "col"), None),
        P("expert", "row", "col"),
        P("expert", "row", "col"),
        P("expert", "col", "row"),
    )
    return jax.shard_map(
        on_device,
        mesh=mesh,
        in_specs=placed,
        out_specs=P(("expert", "col"), "row"),
        check_vma=False,
    )
```

```python
import jax
import jax.numpy as jnp
from jax import lax
from jax.experimental import pallas as pl
from jax.experimental.pallas import tpu as pltpu
from jax.sharding import PartitionSpec as P

MESH = pl.DeviceIdType.MESH
BF16 = jnp.bfloat16
F32 = jnp.float32

N_Y = 4
N_Z = 8
N_X = 4
T_DEV = 64
SUPER = N_Y * T_DEV
N_LOCAL = 4
CAP = N_Y * (5 * T_DEV // 16)
SLOTS = N_LOCAL * CAP
ROWS = 2 * CAP
HALF = ROWS // 2
META = 128
ORDER = (0, 1, 3, 4, 5, 7, 6, 2)


def dot(a, b):
    return jnp.dot(a, b, preferred_element_type=F32)


def dot_nt(a, b):
    return lax.dot_general(a, b, (((1,), (1,)), ((), ())), preferred_element_type=F32)


def kernel(
    tok_ref, ids_ref, rw_ref, wg_hbm, wu_hbm, wd_hbm, out_ref,
    wg, wu, wd, tri, eye, xbuf, table, tableT, sw, rowsbuf, gubuf, r1, r2, hbuf, obuf, keep, ces, cer,
    yb, ry1, ry2, zp, zs, zr,
    wsem, ya_s, ya1_r, ya2_r, gz_s, gz_r, gx_s, gx_r, x_s, x1_r, x2_r, h_s, h1_r, h2_r, ce_s, ce_r,
    y_s, y1_r, y2_r, z_s, z_r,
):
    feat = tok_ref.shape[1]
    hid = wg.shape[2]
    e = lax.axis_index("expert")
    x = lax.axis_index("row")
    c = lax.axis_index("col")
    z = c // N_Y
    y = c % N_Y
    xp, xm, xo = (x + 1) % N_X, (x + 3) % N_X, (x + 2) % N_X
    yp, ym, yo = (y + 1) % N_Y, (y + 3) % N_Y, (y + 2) % N_Y
    zup, zdn = (z + 1) % N_Z, (z + N_Z - 1) % N_Z
    partner = (1 - e, x, c)
    dev_xp, dev_xm = (e, xp, c), (e, xm, c)
    dev_yp, dev_ym = (e, x, z * N_Y + yp), (e, x, z * N_Y + ym)
    dev_zu, dev_zd = (e, x, zup * N_Y + y), (e, x, zdn * N_Y + y)

    def send(src, dst, ssem, rsem, dev):
        return pltpu.make_async_remote_copy(
            src_ref=src, dst_ref=dst, send_sem=ssem, recv_sem=rsem, device_id=dev,
            device_id_type=MESH,
        )

    def landed(dst, rsem):
        send(dst, dst, rsem, rsem, partner).wait_recv()

    def left(src, ssem):
        send(src, src, ssem, ssem, partner).wait_send()

    def place(j):
        off = (j // 2) * (1 - j % 2) - ((j + 1) // 2) * (j % 2)
        return (z + off + N_Z) % N_Z

    def arrival(i):
        j = i
        for at, value in enumerate(ORDER):
            j = jnp.where(i == at, value, j)
        return j

    def chunk(i):
        return place(arrival(i))

    weights = [
        pltpu.make_async_copy(wg_hbm, wg, wsem.at[0]),
        pltpu.make_async_copy(wu_hbm, wu, wsem.at[1]),
        pltpu.make_async_copy(wd_hbm, wd, wsem.at[2]),
    ]
    for copy in weights:
        copy.start()

    barrier = pltpu.get_barrier_semaphore()
    for dev in (partner, dev_xp, dev_xm, dev_yp, dev_ym, dev_zu, dev_zd):
        pl.semaphore_signal(barrier, inc=1, device_id=dev, device_id_type=MESH)

    line = lax.broadcasted_iota(jnp.int32, (META, T_DEV), 0)
    lines = jnp.zeros((META, T_DEV), F32)
    for k in range(2):
        lines = jnp.where(line == k, ids_ref[k : k + 1].astype(F32), lines)
        rest = rw_ref[k : k + 1]
        for part in range(3):
            piece = rest.astype(BF16).astype(F32)
            lines = jnp.where(line == 2 + 3 * k + part, piece, lines)
            rest = rest - piece
    same = (
        lax.broadcasted_iota(jnp.int32, (T_DEV, T_DEV), 0)
        == lax.broadcasted_iota(jnp.int32, (T_DEV, T_DEV), 1)
    ).astype(F32).astype(BF16)
    meta = dot_nt(same, lines.astype(BF16))
    own = xbuf.at[z, e, y]
    xbuf[z, e, y, :, 0:feat] = tok_ref[...]
    xbuf[z, e, y, :, feat : feat + META] = meta.astype(BF16)

    across = lax.broadcasted_iota(jnp.int32, (SUPER, SUPER), 0)
    along = lax.broadcasted_iota(jnp.int32, (SUPER, SUPER), 1)
    tri[...] = (across < along).astype(F32).astype(BF16)
    eye[...] = (across == along).astype(F32).astype(BF16)

    pl.semaphore_wait(barrier, 7)

    half = T_DEV // 2
    low, high = pl.ds(0, half), pl.ds(half, half)

    def hop_gz(at):
        j, up = (0, at == 0) if at in (0, 7) else (at, at % 2 == 1)
        part = xbuf.at[place(j), e, y]
        to = j + 2 if j else (1 if up else 2)
        if j > 4:
            part, to = part.at[low if up else high], (7 if up else 8)
        return send(part, part, gz_s.at[at], gz_r.at[to], dev_zu if up else dev_zd)

    def z_pass(j):
        block = xbuf.at[place(j), e, y]
        if j == 7:
            landed(block.at[low], gz_r.at[7])
            landed(block.at[high], gz_r.at[8])
            return
        landed(block, gz_r.at[j])
        hop_gz(j).start()
        landed(xbuf.at[place(j + 1), e, y], gz_r.at[j + 1])
        hop_gz(j + 1).start()

    def hop_ya1(k, zc):
        block = xbuf.at[zc, e, y]
        return (
            send(block, block, ya_s.at[k], ya1_r.at[k], dev_yp),
            send(block, block, ya_s.at[k], ya1_r.at[k], dev_ym),
        )

    def hop_ya2(k, zc):
        a, b = xbuf.at[zc, e, ym, low], xbuf.at[zc, e, yp, high]
        return (
            send(a, a, ya_s.at[k], ya2_r.at[k], dev_yp),
            send(b, b, ya_s.at[k], ya2_r.at[k], dev_ym),
        )

    def hop_gx(k, zc):
        block = xbuf.at[zc, e]
        return send(block, block, gx_s.at[k], gx_r.at[k], partner)

    def stage_y1(k, zc):
        for copy in hop_ya1(k, zc):
            copy.start()

    def stage_y2(k, zc):
        landed(xbuf.at[zc, e, pl.ds(0, 2)], ya1_r.at[k])
        for copy in hop_ya2(k, zc):
            copy.start()

    def stage_y3(k, zc):
        landed(xbuf.at[zc, e, yo], ya2_r.at[k])
        hop_gx(k, zc).start()

    stage_y1(0, z)
    hop_gz(0).start()
    hop_gz(7).start()
    stage_y2(0, z)
    z_pass(1)
    stage_y1(1, place(ORDER[1]))
    stage_y3(0, z)
    for copy in weights:
        copy.wait()

    def stage_a1(i, zc):
        par = lax.rem(i, 3)
        landed(xbuf.at[zc, 1 - e], gx_r.at[i])
        pick = (
            lax.broadcasted_iota(jnp.int32, (16, META), 0)
            == lax.broadcasted_iota(jnp.int32, (16, META), 1)
        ).astype(F32).astype(BF16)
        ex = lax.broadcasted_iota(jnp.int32, (8, SUPER), 0).astype(F32)
        slot = lax.broadcasted_iota(jnp.int32, (CAP, SUPER), 0).astype(F32)
        base = (e * N_LOCAL).astype(F32)
        for s in range(2):
            info = xbuf[zc, s, :, :, feat : feat + META].reshape(SUPER, META)
            rows = dot_nt(pick, info)
            id0 = rows[0:1] - base
            id1 = rows[1:2] - base
            w0 = rows[2:3] + rows[3:4] + rows[4:5]
            w1 = rows[5:6] + rows[6:7] + rows[7:8]
            member = jnp.logical_or(ex == id0, ex == id1).astype(F32)
            rank = dot(member.astype(BF16), tri[...])
            rank = jnp.where(member > 0.5, rank, -1.0)
            for v in range(N_LOCAL):
                hit = (rank[v : v + 1] == slot).astype(F32)
                share = jnp.where(id0 == v, w0, 0.0) + jnp.where(id1 == v, w1, 0.0)
                table[par, s, v * CAP : (v + 1) * CAP, :] = hit.astype(BF16)
                sw[par, v, s * CAP : (s + 1) * CAP, :] = jnp.broadcast_to(
                    jnp.sum(hit * share, axis=1, keepdims=True), (CAP, 128)
                )
            tableT[par, s] = dot_nt(eye[...], table[par, s]).astype(BF16)
            for n in range(0, feat, 256):
                got = dot(
                    table[par, s], xbuf[zc, s, :, :, n : n + 256].reshape(SUPER, 256)
                ).astype(BF16)
                for v in range(N_LOCAL):
                    rowsbuf[v, s * CAP : (s + 1) * CAP, n : n + 256] = got[
                        v * CAP : (v + 1) * CAP
                    ]

    def stage_a2(i):
        par = lax.rem(i, 2)

        def up_one(v, carry):
            rows = rowsbuf[v]
            gubuf[par, v, :, 0:hid] = dot(rows, wg[v]).astype(BF16)
            gubuf[par, v, :, hid : 2 * hid] = dot(rows, wu[v]).astype(BF16)
            return carry

        lax.fori_loop(0, N_LOCAL, up_one, 0, unroll=True)
        for copy in hop_x1(i):
            copy.start()

    top, bot = pl.ds(0, HALF), pl.ds(HALF, HALF)

    def hop_x1(i):
        g = gubuf.at[lax.rem(i, 2)]
        return (
            send(g.at[xo, top], r1.at[i, 0], x_s.at[i], x1_r.at[i], dev_xp),
            send(g.at[xo, bot], r1.at[i, 1], x_s.at[i], x1_r.at[i], dev_xm),
        )

    def hop_x2(i):
        g = gubuf.at[lax.rem(i, 2)]
        return (
            send(g.at[xp], r2.at[i, 0], x_s.at[i], x2_r.at[i], dev_xp),
            send(g.at[xm], r2.at[i, 1], x_s.at[i], x2_r.at[i], dev_xm),
        )

    def stage_c(i):
        par = lax.rem(i, 2)
        to_p, to_m = hop_x2(i)
        landed(r1.at[i], x1_r.at[i])
        gubuf[par, xp, top] = (
            gubuf[par, xp, top].astype(F32) + r1[i, 0].astype(F32)
        ).astype(BF16)
        to_p.start()
        gubuf[par, xm, bot] = (
            gubuf[par, xm, bot].astype(F32) + r1[i, 1].astype(F32)
        ).astype(BF16)
        to_m.start()

    def hop_h1(i):
        mine = hbuf.at[i, x]
        return (
            send(mine, mine, h_s.at[i], h1_r.at[i], dev_xp),
            send(mine, mine, h_s.at[i], h1_r.at[i], dev_xm),
        )

    def hop_h2(i):
        a, b = hbuf.at[i, xm, top], hbuf.at[i, xp, bot]
        return (
            send(a, a, h_s.at[i], h2_r.at[i], dev_xp),
            send(b, b, h_s.at[i], h2_r.at[i], dev_xm),
        )

    def stage_b(i):
        par = lax.rem(i, 2)
        landed(r2.at[i], x2_r.at[i])
        total = (
            gubuf[par, x].astype(F32) + r2[i, 0].astype(F32) + r2[i, 1].astype(F32)
        )
        gate, up = total[:, 0:hid], total[:, hid : 2 * hid]
        hbuf[i, x] = (gate / (1.0 + jnp.exp(-gate)) * up).astype(BF16)
        for copy in hop_h1(i):
            copy.start()
        left(gubuf.at[par, pl.ds(0, 3)], x_s.at[i])

    def stage_d(i):
        to_p, to_m = hop_h2(i)
        landed(hbuf.at[i, pl.ds(0, 2)], h1_r.at[i])
        to_p.start()
        to_m.start()

    def hop_ce(i):
        return send(ces, cer.at[i], ce_s.at[i], ce_r.at[i], partner)

    def stage_e1(i):
        par = lax.rem(i, 3)
        landed(hbuf.at[i, xo], h2_r.at[i])

        def down_one(v, carry):
            scale = jnp.concatenate([sw[par, v], sw[par, v]], axis=1)
            for n in range(0, feat, 256):
                res = (dot(hbuf[i, v], wd[v, :, n : n + 256]) * scale).astype(BF16)
                for s in range(2):
                    obuf[s, pl.ds(pl.multiple_of(v * CAP, CAP), CAP), n : n + 256] = res[
                        s * CAP : (s + 1) * CAP
                    ]
            return carry

        lax.fori_loop(0, N_LOCAL, down_one, 0, unroll=True)

    def stage_e2(i):
        par = lax.rem(i, 3)
        for n in range(0, feat, 256):
            ces[:, n : n + 256] = dot(
                tableT[par, 1 - e], obuf[1 - e, :, n : n + 256]
            ).astype(BF16)
        hop_ce(i).start()
        for n in range(0, feat, 256):
            keep[:, n : n + 256] = dot(tableT[par, e], obuf[e, :, n : n + 256])
        left(hbuf.at[i, pl.ds(0, 3)], h_s.at[i])

    def hop_y1(i):
        return (
            send(yb.at[lax.rem(i, 2), yo, low], ry1.at[i, 0], y_s.at[i], y1_r.at[i], dev_yp),
            send(yb.at[lax.rem(i, 2), yo, high], ry1.at[i, 1], y_s.at[i], y1_r.at[i], dev_ym),
        )

    def hop_y2(i):
        return (
            send(yb.at[lax.rem(i, 2), yp], ry2.at[i, 0], y_s.at[i], y2_r.at[i], dev_yp),
            send(yb.at[lax.rem(i, 2), ym], ry2.at[i, 1], y_s.at[i], y2_r.at[i], dev_ym),
        )

    def stage_f(i):
        par = lax.rem(i, 2)
        hop = hop_ce(i)
        hop.wait_recv()
        for b in range(N_Y):
            part = slice(b * T_DEV, (b + 1) * T_DEV)
            yb[par, b] = (keep[part] + cer[i, part].astype(F32)).astype(BF16)
        for copy in hop_y1(i):
            copy.start()
        hop.wait_send()

    def stage_g(i):
        par = lax.rem(i, 2)
        to_p, to_m = hop_y2(i)
        landed(ry1.at[i], y1_r.at[i])
        yb[par, yp, low] = (yb[par, yp, low].astype(F32) + ry1[i, 0].astype(F32)).astype(BF16)
        to_p.start()
        yb[par, ym, high] = (yb[par, ym, high].astype(F32) + ry1[i, 1].astype(F32)).astype(BF16)
        to_m.start()

    def stage_h(i, zc):
        par = lax.rem(i, 2)
        landed(ry2.at[i], y2_r.at[i])
        zp[zc] = yb[par, y].astype(F32) + ry2[i, 0].astype(F32) + ry2[i, 1].astype(F32)
        left(yb.at[par, pl.ds(0, 3)], y_s.at[i])

    def hop_z(k, way):
        dev = dev_zd if way == 0 else dev_zu
        part = zs.at[way, k]
        into = zr.at[way, k]
        if k == 0:
            rows = low if way == 0 else high
            part, into = part.at[rows], into.at[rows]
        return send(part, into, z_s.at[way, k], z_r.at[way, k], dev)

    def stage_z(k, way):
        far = 4 - k
        dest = (z + (N_Z - far if way == 0 else far)) % N_Z
        rows, other = (low, high) if way == 0 else (high, low)
        if k == 0:
            zs[way, k, rows] = zp[dest, rows].astype(BF16)
        elif k == 1:
            landed(zr.at[way, 0, rows], z_r.at[way, 0])
            zs[way, k, other] = zp[dest, other].astype(BF16)
            zs[way, k, rows] = (zp[dest, rows] + zr[way, 0, rows].astype(F32)).astype(BF16)
        else:
            landed(zr.at[way, k - 1], z_r.at[way, k - 1])
            zs[way, k] = (zp[dest] + zr[way, k - 1].astype(F32)).astype(BF16)
        hop_z(k, way).start()

    def body(i, zcs):
        def at(lag, stage, located=False):
            @pl.when(jnp.logical_and(i >= lag, i < N_Z + lag))
            def _():
                stage(*((i - lag, zcs[lag + 2]) if located else (i - lag,)))

        def once(when, stage, *given):
            @pl.when(i == when)
            def _():
                stage(*given)

        @pl.when(jnp.logical_and(i > 0, i < N_Z - 2))
        def _():
            stage_y1(i + 2, zcs[0])

        once(N_Z + 4, stage_z, 2, 0)
        once(N_Z + 4, stage_z, 2, 1)
        at(0, stage_a1, True)
        once(0, stage_y2, 1, place(ORDER[1]))
        once(0, z_pass, 3)
        once(0, stage_y1, 2, zcs[0])
        at(5, stage_h, True)
        for k in range(2):
            once(N_Z + 2 + k, stage_z, k, 0)
            once(N_Z + 2 + k, stage_z, k, 1)
        at(2, stage_d)
        at(0, stage_a2)
        once(0, z_pass, 5)
        once(1, z_pass, 7)
        at(4, stage_g)
        at(-1, stage_y3, True)
        at(3, stage_f)
        at(1, stage_b)
        at(2, stage_e1)
        at(-2, stage_y2, True)
        at(0, stage_c)
        at(2, stage_e2)
        return (chunk(i + 3),) + zcs[:-1]

    lax.fori_loop(0, N_Z + 5, body, (place(ORDER[2]), place(ORDER[1])) + (z,) * 6)
    stage_z(3, 0)
    stage_z(3, 1)
    landed(zr.at[0, 3], z_r.at[0, 3])
    landed(zr.at[1, 3], z_r.at[1, 3])
    out_ref[...] = (zp[z] + zr[0, 3].astype(F32) + zr[1, 3].astype(F32)).astype(BF16)
    for k in range(4):
        for way in range(2):
            hop_z(k, way).wait_send()

    for at in range(8):
        hop_gz(at).wait_send()

    def gone(k, carry):
        left(xbuf.at[z, e, pl.ds(0, 3)], ya_s.at[k])
        left(xbuf.at[z, e], gx_s.at[k])
        return carry

    lax.fori_loop(0, N_Z, gone, 0)


def on_device(tokens, expert_ids, route_weight, gate_w, up_w, down_w):
    t_dev, feat = tokens.shape
    n_local, _, hid = gate_w.shape
    vmem = pl.BlockSpec(memory_space=pltpu.VMEM)
    hbm = pl.BlockSpec(memory_space=pl.ANY)
    dma = pltpu.SemaphoreType.DMA
    wide = feat + META
    return pl.pallas_call(
        kernel,
        out_shape=jax.ShapeDtypeStruct((t_dev, feat), BF16),
        in_specs=[vmem, vmem, vmem, hbm, hbm, hbm],
        out_specs=vmem,
        scratch_shapes=[
            pltpu.VMEM((n_local, feat, hid), BF16),
            pltpu.VMEM((n_local, feat, hid), BF16),
            pltpu.VMEM((n_local, hid, feat), BF16),
            pltpu.VMEM((SUPER, SUPER), BF16),
            pltpu.VMEM((SUPER, SUPER), BF16),
            pltpu.VMEM((N_Z, 2, N_Y, T_DEV, wide), BF16),
            pltpu.VMEM((3, 2, SLOTS, SUPER), BF16),
            pltpu.VMEM((3, 2, SUPER, SLOTS), BF16),
            pltpu.VMEM((3, N_LOCAL, ROWS, 128), F32),
            pltpu.VMEM((N_LOCAL, ROWS, feat), BF16),
            pltpu.VMEM((2, N_LOCAL, ROWS, 2 * hid), BF16),
            pltpu.VMEM((N_Z, 2, HALF, 2 * hid), BF16),
            pltpu.VMEM((N_Z, 2, ROWS, 2 * hid), BF16),
            pltpu.VMEM((N_Z, N_LOCAL, ROWS, hid), BF16),
            pltpu.VMEM((2, SLOTS, feat), BF16),
            pltpu.VMEM((SUPER, feat), F32),
            pltpu.VMEM((SUPER, feat), BF16),
            pltpu.VMEM((N_Z, SUPER, feat), BF16),
            pltpu.VMEM((2, N_Y, T_DEV, feat), BF16),
            pltpu.VMEM((N_Z, 2, T_DEV // 2, feat), BF16),
            pltpu.VMEM((N_Z, 2, T_DEV, feat), BF16),
            pltpu.VMEM((N_Z, T_DEV, feat), F32),
            pltpu.VMEM((2, 4, T_DEV, feat), BF16),
            pltpu.VMEM((2, 4, T_DEV, feat), BF16),
            dma((3,)),
            dma((8,)), dma((8,)), dma((8,)),
            dma((8,)), dma((9,)),
            dma((8,)), dma((8,)),
            dma((8,)), dma((8,)), dma((8,)),
            dma((8,)), dma((8,)), dma((8,)),
            dma((8,)), dma((8,)),
            dma((8,)), dma((8,)), dma((8,)),
            dma((2, 4)), dma((2, 4)),
        ],
        compiler_params=pltpu.CompilerParams(
            collective_id=0, has_side_effects=True, vmem_limit_bytes=58 * 1024 * 1024
        ),
        cost_estimate=pl.CostEstimate(
            flops=12_000_000_000, bytes_accessed=8_000_000, transcendentals=2_000_000
        ),
        name="moe_layer",
    )(tokens, expert_ids.T, route_weight.T, gate_w, up_w, down_w)


def solution(mesh):
    placed = (
        P(("expert", "col"), "row"),
        P(("expert", "col"), None),
        P(("expert", "col"), None),
        P("expert", "row", "col"),
        P("expert", "row", "col"),
        P("expert", "col", "row"),
    )
    return jax.shard_map(
        on_device,
        mesh=mesh,
        in_specs=placed,
        out_specs=P(("expert", "col"), "row"),
        check_vma=False,
    )
```

```python
import jax
import jax.numpy as jnp
from jax import lax
from jax.experimental import pallas as pl
from jax.experimental.pallas import tpu as pltpu
from jax.sharding import PartitionSpec as P

MESH = pl.DeviceIdType.MESH
BF16 = jnp.bfloat16
F32 = jnp.float32

N_Y = 4
N_Z = 8
N_X = 4
T_DEV = 64
SUPER = N_Y * T_DEV
EXPERTS = 8
N_LOCAL = 4
CAP = N_Y * (5 * T_DEV // 16)
SLOTS = EXPERTS * CAP
PAIRS = 2 * SUPER
SHARD = PAIRS // N_X
HALF = SHARD // 2
META = 128
ORDER = (0, 1, 5, 7, 6, 3, 4, 2)
PLAN = (
    "a10 zp2 a20 y21",
    "zp3 y12 c0 a11",
    "a21 y22 zp4 y13",
    "y14 b0 c1 a12",
    "d0 a22 y23 y15",
    "b1 e10 y24 e20",
    "c2 a13 d1 a23",
    "y16 y25 a14 e11",
    "c3 b2 a24 y17",
    "y26 g0 e21 b3",
    "a15 d2 a25 c4",
    "d3 e12 h0 y27",
    "e22 c5 g1 a16",
    "a26 e13 b4 h1",
    "b5 g2 c6 e23",
    "a17 d4 a27 h2",
    "d5 g3 b6 e14",
    "c7 e24 h3 zr0",
    "d6 e15 e25 b7",
    "e16 g4 e26 d7",
    "g5 h4 zr1 e17",
    "g6 e27 h5 h6",
    "zr2 g7 h7 zr3",
)
TABLES = 4
SUMS = 4


def dot(a, b):
    return jnp.dot(a, b, preferred_element_type=F32)


def dot_nt(a, b):
    return lax.dot_general(a, b, (((1,), (1,)), ((), ())), preferred_element_type=F32)


def same(n):
    one = lax.broadcasted_iota(jnp.int32, (n, n), 0) == lax.broadcasted_iota(jnp.int32, (n, n), 1)
    return one.astype(F32).astype(BF16)


def kernel(
    tok_hbm, ids_hbm, rw_hbm, wg_hbm, wu_hbm, wd_hbm, out_ref,
    ids_ref, rw_ref, wg, wu, wd, tri, eye, xbuf, hits, pairs, back, mix, rowsbuf, both, gubuf,
    r1, r2, hbuf, hs, obuf, yb, ry1, ry2, zp, zs, zr,
    in_sem, w_sem, ws_s, ws_r, ya_s, ya1_r, ya2_r, gz_s, gz_r, x_s, x1_r, x2_r, h_s, h1_r, h2_r,
    y_s, y1_r, y2_r, z_s, z_r,
):
    feat = tok_hbm.shape[1]
    hid = wg.shape[2]
    e = lax.axis_index("expert")
    x = lax.axis_index("row")
    c = lax.axis_index("col")
    z = c // N_Y
    y = c % N_Y
    xp, xm, xo = (x + 1) % N_X, (x + 3) % N_X, (x + 2) % N_X
    yp, ym, yo = (y + 1) % N_Y, (y + 3) % N_Y, (y + 2) % N_Y
    zup, zdn = (z + 1) % N_Z, (z + N_Z - 1) % N_Z
    partner = (1 - e, x, c)
    dev_xp, dev_xm = (e, xp, c), (e, xm, c)
    dev_yp, dev_ym = (e, x, z * N_Y + yp), (e, x, z * N_Y + ym)
    dev_zu, dev_zd = (e, x, zup * N_Y + y), (e, x, zdn * N_Y + y)

    barrier = pltpu.get_barrier_semaphore()
    for dev in (partner, dev_xp, dev_xm, dev_yp, dev_ym, dev_zu, dev_zd):
        pl.semaphore_signal(barrier, inc=1, device_id=dev, device_id_type=MESH)

    own = xbuf.at[z, y]
    inputs = (
        pltpu.make_async_copy(ids_hbm, ids_ref, in_sem.at[0]),
        pltpu.make_async_copy(rw_hbm, rw_ref, in_sem.at[1]),
        pltpu.make_async_copy(tok_hbm, own.at[:, pl.ds(0, feat)], in_sem.at[2]),
    )
    for copy in inputs:
        copy.start()
    mine = pl.ds(e * N_LOCAL, N_LOCAL)
    theirs = pl.ds((1 - e) * N_LOCAL, N_LOCAL)
    loads = []
    for n, (src, dst) in enumerate(((wg_hbm, wg), (wu_hbm, wu), (wd_hbm, wd))):
        loads.append(pltpu.make_async_copy(src, dst.at[mine], w_sem.at[n]))
        loads[-1].start()

    def send(src, dst, ssem, rsem, dev):
        return pltpu.make_async_remote_copy(
            src_ref=src, dst_ref=dst, send_sem=ssem, recv_sem=rsem, device_id=dev,
            device_id_type=MESH,
        )

    def landed(dst, rsem):
        send(dst, dst, rsem, rsem, partner).wait_recv()

    def left(src, ssem):
        send(src, src, ssem, ssem, partner).wait_send()

    def place(j):
        off = (j // 2) * (1 - j % 2) - ((j + 1) // 2) * (j % 2)
        return (z + off + N_Z) % N_Z

    def chunk(i):
        return place(ORDER[i])

    across = lax.broadcasted_iota(jnp.int32, (SUPER, SUPER), 0)
    along = lax.broadcasted_iota(jnp.int32, (SUPER, SUPER), 1)
    tri[...] = (across < along).astype(F32).astype(BF16)
    eye[...] = same(SUPER)

    inputs[0].wait()
    inputs[1].wait()
    line = lax.broadcasted_iota(jnp.int32, (META, T_DEV), 0)
    lines = jnp.zeros((META, T_DEV), F32)
    for k in range(2):
        lines = jnp.where(line == k, ids_ref[k : k + 1].astype(F32), lines)
        rest = rw_ref[k : k + 1]
        for part in range(3):
            piece = rest.astype(BF16).astype(F32)
            lines = jnp.where(line == 2 + 3 * k + part, piece, lines)
            rest = rest - piece
    xbuf[z, y, :, feat : feat + META] = dot_nt(same(T_DEV), lines.astype(BF16)).astype(BF16)
    inputs[2].wait()

    pl.semaphore_wait(barrier, 7)

    half = T_DEV // 2
    low, high = pl.ds(0, half), pl.ds(half, half)

    def hop_gz(at):
        j, up = (0, at == 0) if at in (0, 7) else (at, at % 2 == 1)
        part = xbuf.at[place(j), y]
        to = j + 2 if j else (1 if up else 2)
        if j > 4:
            part, to = part.at[low if up else high], (7 if up else 8)
        return send(part, part, gz_s.at[at], gz_r.at[to], dev_zu if up else dev_zd)

    def stage_zp(k):
        j = 2 * k - 1
        block = xbuf.at[place(j), y]
        if j == 7:
            landed(block.at[low], gz_r.at[7])
            landed(block.at[high], gz_r.at[8])
            return
        landed(block, gz_r.at[j])
        hop_gz(j).start()
        landed(xbuf.at[place(j + 1), y], gz_r.at[j + 1])
        hop_gz(j + 1).start()

    def stage_y1(k):
        block = xbuf.at[chunk(k), y]
        send(block, block, ya_s.at[k], ya1_r.at[k], dev_yp).start()
        send(block, block, ya_s.at[k], ya1_r.at[k], dev_ym).start()

    def stage_y2(k):
        zc = chunk(k)
        landed(xbuf.at[zc, pl.ds(0, 2)], ya1_r.at[k])
        a, b = xbuf.at[zc, ym, low], xbuf.at[zc, yp, high]
        send(a, a, ya_s.at[k], ya2_r.at[k], dev_yp).start()
        send(b, b, ya_s.at[k], ya2_r.at[k], dev_ym).start()

    def to_partner(n):
        src, dst = ((wg_hbm, wg), (wu_hbm, wu), (wd_hbm, wd))[n]
        return send(src, dst.at[mine], ws_s.at[n], ws_r.at[n], partner)

    stage_y1(0)
    hop_gz(0).start()
    hop_gz(7).start()
    for n in range(3):
        to_partner(n).start()
    stage_y2(0)
    stage_zp(1)
    stage_y1(1)
    for copy in loads:
        copy.wait()

    def stage_a1(i):
        zc = chunk(i)
        par = i % TABLES
        landed(xbuf.at[zc, yo], ya2_r.at[i])
        pick = (
            lax.broadcasted_iota(jnp.int32, (16, META), 0)
            == lax.broadcasted_iota(jnp.int32, (16, META), 1)
        ).astype(F32).astype(BF16)
        info = xbuf[zc, :, :, feat : feat + META].reshape(SUPER, META)
        rows = dot_nt(pick, info)
        id0, id1 = rows[0:1], rows[1:2]
        ex = lax.broadcasted_iota(jnp.int32, (EXPERTS, SUPER), 0).astype(F32)
        slot = lax.broadcasted_iota(jnp.int32, (CAP, SUPER), 0).astype(F32)
        member = jnp.logical_or(ex == id0, ex == id1)
        rank = dot(member.astype(F32).astype(BF16), tri[...])
        rank = jnp.where(member, rank, -1.0)
        for v in range(EXPERTS):
            rows_v = slice(v * CAP, (v + 1) * CAP)
            hit = (rank[v : v + 1] == slot).astype(F32)
            first = jnp.where(id0 == v, hit, 0.0)
            hits[rows_v, :] = hit.astype(BF16)
            pairs[par, rows_v, 0:SUPER] = first.astype(BF16)
            pairs[par, rows_v, SUPER:PAIRS] = (hit - first).astype(BF16)
        for n in range(0, feat, 256):
            rowsbuf[:, n : n + 256] = dot(
                hits[...], xbuf[zc, :, :, n : n + 256].reshape(SUPER, 256)
            ).astype(BF16)
        one = dot_nt(eye[...], pairs[par, :, 0:SUPER])
        two = dot_nt(eye[...], pairs[par, :, SUPER:PAIRS])
        back[0:SUPER] = one.astype(BF16)
        back[SUPER:PAIRS] = two.astype(BF16)
        mix[par] = (one + two).astype(BF16)

    def stage_a2(i):
        par = i % SUMS
        for n in range(EXPERTS):
            if i == 0:
                if n == N_LOCAL:
                    landed(wg.at[theirs], ws_r.at[0])
                    landed(wu.at[theirs], ws_r.at[1])
                v = (e * N_LOCAL + n) % EXPERTS
                rows_v = pl.ds(pl.multiple_of(v * CAP, 16), CAP)
            else:
                v, rows_v = n, slice(n * CAP, (n + 1) * CAP)
            rows = rowsbuf[rows_v, :]
            both[rows_v, 0:hid] = dot(rows, wg[v]).astype(BF16)
            both[rows_v, hid : 2 * hid] = dot(rows, wu[v]).astype(BF16)
        for n in range(0, 2 * hid, 256):
            gubuf[par, :, :, n : n + 256] = (
                dot(back[...], both[:, n : n + 256]).astype(BF16).reshape(N_X, SHARD, 256)
            )
        g = gubuf.at[par]
        send(g.at[xo, top], r1.at[i, 0], x_s.at[i], x1_r.at[i], dev_xp).start()
        send(g.at[xo, bot], r1.at[i, 1], x_s.at[i], x1_r.at[i], dev_xm).start()

    top, bot = pl.ds(0, HALF), pl.ds(HALF, HALF)

    def stage_c(i):
        par = i % SUMS
        g = gubuf.at[par]
        landed(r1.at[i], x1_r.at[i])
        gubuf[par, xp, top] = (
            gubuf[par, xp, top].astype(F32) + r1[i, 0].astype(F32)
        ).astype(BF16)
        send(g.at[xp], r2.at[i, 0], x_s.at[i], x2_r.at[i], dev_xp).start()
        gubuf[par, xm, bot] = (
            gubuf[par, xm, bot].astype(F32) + r1[i, 1].astype(F32)
        ).astype(BF16)
        send(g.at[xm], r2.at[i, 1], x_s.at[i], x2_r.at[i], dev_xm).start()

    def stage_b(i):
        par = i % SUMS
        landed(r2.at[i], x2_r.at[i])
        total = gubuf[par, x].astype(F32) + r2[i, 0].astype(F32) + r2[i, 1].astype(F32)
        gate, up = total[:, 0:hid], total[:, hid : 2 * hid]
        info = xbuf[chunk(i), pl.ds((x % 2) * 2, 2), :, feat : feat + META]
        info = info.reshape(SHARD, META).astype(F32)
        w0 = info[:, 2:3] + info[:, 3:4] + info[:, 4:5]
        w1 = info[:, 5:6] + info[:, 6:7] + info[:, 7:8]
        weight = jnp.where(x // 2 == 1, w1, w0)
        hbuf[i, x] = (gate / (1.0 + jnp.exp(-gate)) * up * weight).astype(BF16)
        block = hbuf.at[i, x]
        send(block, block, h_s.at[i], h1_r.at[i], dev_xp).start()
        send(block, block, h_s.at[i], h1_r.at[i], dev_xm).start()
        left(gubuf.at[par, pl.ds(0, 3)], x_s.at[i])

    def stage_d(i):
        landed(hbuf.at[i, pl.ds(0, 2)], h1_r.at[i])
        a, b = hbuf.at[i, xm, top], hbuf.at[i, xp, bot]
        send(a, a, h_s.at[i], h2_r.at[i], dev_xp).start()
        send(b, b, h_s.at[i], h2_r.at[i], dev_xm).start()

    def stage_e1(i):
        landed(hbuf.at[i, xo], h2_r.at[i])
        if i == 0:
            landed(wd.at[theirs], ws_r.at[2])
        hs[...] = dot(pairs[i % TABLES], hbuf[i].reshape(PAIRS, hid)).astype(BF16)
        for v in range(EXPERTS):
            rows_v = slice(v * CAP, (v + 1) * CAP)
            for n in range(0, feat, 256):
                obuf[rows_v, n : n + 256] = dot(hs[rows_v, :], wd[v, :, n : n + 256]).astype(BF16)

    def stage_e2(i):
        block = yb.at[i % 3]
        for n in range(0, feat, 256):
            part = dot(mix[i % TABLES], obuf[:, n : n + 256])
            yb[i % 3, :, :, n : n + 256] = part.astype(BF16).reshape(N_Y, T_DEV, 256)
        send(block.at[yo, low], ry1.at[i, 0], y_s.at[i], y1_r.at[i], dev_yp).start()
        send(block.at[yo, high], ry1.at[i, 1], y_s.at[i], y1_r.at[i], dev_ym).start()
        send(block.at[yp, high], ry2.at[i, 0, high], y_s.at[i], y2_r.at[i], dev_yp).start()
        send(block.at[ym, low], ry2.at[i, 1, low], y_s.at[i], y2_r.at[i], dev_ym).start()

    def stage_g(i):
        par = i % 3
        block = yb.at[par]
        landed(ry1.at[i], y1_r.at[i])
        yb[par, yp, low] = (yb[par, yp, low].astype(F32) + ry1[i, 0].astype(F32)).astype(BF16)
        send(block.at[yp, low], ry2.at[i, 0, low], y_s.at[i], y2_r.at[i], dev_yp).start()
        yb[par, ym, high] = (yb[par, ym, high].astype(F32) + ry1[i, 1].astype(F32)).astype(BF16)
        send(block.at[ym, high], ry2.at[i, 1, high], y_s.at[i], y2_r.at[i], dev_ym).start()

    def stage_h(i):
        par = i % 3
        landed(ry2.at[i], y2_r.at[i])
        zp[chunk(i)] = yb[par, y].astype(F32) + ry2[i, 0].astype(F32) + ry2[i, 1].astype(F32)
        left(yb.at[par, pl.ds(0, 3)], y_s.at[i])

    def hop_z(k, way):
        dev = dev_zd if way == 0 else dev_zu
        part = zs.at[way, k]
        into = zr.at[way, k]
        if k == 0:
            rows = low if way == 0 else high
            part, into = part.at[rows], into.at[rows]
        return send(part, into, z_s.at[way, k], z_r.at[way, k], dev)

    def stage_zr(k):
        for way in range(2):
            far = 4 - k
            dest = (z + (N_Z - far if way == 0 else far)) % N_Z
            rows, other = (low, high) if way == 0 else (high, low)
            if k == 0:
                zs[way, k, rows] = zp[dest, rows].astype(BF16)
            elif k == 1:
                landed(zr.at[way, 0, rows], z_r.at[way, 0])
                zs[way, k, other] = zp[dest, other].astype(BF16)
                zs[way, k, rows] = (zp[dest, rows] + zr[way, 0, rows].astype(F32)).astype(BF16)
            else:
                landed(zr.at[way, k - 1], z_r.at[way, k - 1])
                zs[way, k] = (zp[dest] + zr[way, k - 1].astype(F32)).astype(BF16)
            hop_z(k, way).start()

    stages = dict(
        y1=stage_y1, y2=stage_y2, a1=stage_a1, a2=stage_a2, b=stage_b, c=stage_c,
        d=stage_d, e1=stage_e1, e2=stage_e2, g=stage_g, h=stage_h, zp=stage_zp, zr=stage_zr,
    )
    for line_of_plan in PLAN:
        for step in line_of_plan.split():
            stages[step[:-1]](int(step[-1]))

    landed(zr.at[0, 3], z_r.at[0, 3])
    landed(zr.at[1, 3], z_r.at[1, 3])
    out_ref[...] = (zp[z] + zr[0, 3].astype(F32) + zr[1, 3].astype(F32)).astype(BF16)

    for k in range(4):
        for way in range(2):
            hop_z(k, way).wait_send()
    for at in range(8):
        hop_gz(at).wait_send()
    for n in range(3):
        to_partner(n).wait_send()
    for k in range(N_Z):
        left(xbuf.at[z, pl.ds(0, 3)], ya_s.at[k])
        left(hbuf.at[k, pl.ds(0, 3)], h_s.at[k])


def on_device(tokens, expert_ids, route_weight, gate_w, up_w, down_w):
    t_dev, feat = tokens.shape
    hid = gate_w.shape[2]
    hbm = pl.BlockSpec(memory_space=pl.ANY)
    dma = pltpu.SemaphoreType.DMA
    eight = dma((8,))
    return pl.pallas_call(
        kernel,
        out_shape=jax.ShapeDtypeStruct((t_dev, feat), BF16),
        in_specs=[hbm] * 6,
        out_specs=pl.BlockSpec(memory_space=pltpu.VMEM),
        scratch_shapes=[
            pltpu.VMEM((2, t_dev), jnp.int32),
            pltpu.VMEM((2, t_dev), F32),
            pltpu.VMEM((EXPERTS, feat, hid), BF16),
            pltpu.VMEM((EXPERTS, feat, hid), BF16),
            pltpu.VMEM((EXPERTS, hid, feat), BF16),
            pltpu.VMEM((SUPER, SUPER), BF16),
            pltpu.VMEM((SUPER, SUPER), BF16),
            pltpu.VMEM((N_Z, N_Y, T_DEV, feat + META), BF16),
            pltpu.VMEM((SLOTS, SUPER), BF16),
            pltpu.VMEM((TABLES, SLOTS, PAIRS), BF16),
            pltpu.VMEM((PAIRS, SLOTS), BF16),
            pltpu.VMEM((TABLES, SUPER, SLOTS), BF16),
            pltpu.VMEM((SLOTS, feat), BF16),
            pltpu.VMEM((SLOTS, 2 * hid), BF16),
            pltpu.VMEM((SUMS, N_X, SHARD, 2 * hid), BF16),
            pltpu.VMEM((N_Z, 2, HALF, 2 * hid), BF16),
            pltpu.VMEM((N_Z, 2, SHARD, 2 * hid), BF16),
            pltpu.VMEM((N_Z, N_X, SHARD, hid), BF16),
            pltpu.VMEM((SLOTS, hid), BF16),
            pltpu.VMEM((SLOTS, feat), BF16),
            pltpu.VMEM((3, N_Y, T_DEV, feat), BF16),
            pltpu.VMEM((N_Z, 2, T_DEV // 2, feat), BF16),
            pltpu.VMEM((N_Z, 2, T_DEV, feat), BF16),
            pltpu.VMEM((N_Z, T_DEV, feat), F32),
            pltpu.VMEM((2, 4, T_DEV, feat), BF16),
            pltpu.VMEM((2, 4, T_DEV, feat), BF16),
            dma((3,)), dma((3,)), dma((3,)), dma((3,)),
            eight, eight, eight,
            eight, dma((9,)),
            eight, eight, eight,
            eight, eight, eight,
            eight, eight, eight,
            dma((2, 4)), dma((2, 4)),
        ],
        compiler_params=pltpu.CompilerParams(
            collective_id=0, has_side_effects=True, vmem_limit_bytes=58 * 1024 * 1024
        ),
        cost_estimate=pl.CostEstimate(
            flops=14_000_000_000, bytes_accessed=8_000_000, transcendentals=2_000_000
        ),
        name="moe_layer",
    )(tokens, expert_ids.T, route_weight.T, gate_w, up_w, down_w)


def solution(mesh):
    placed = (
        P(("expert", "col"), "row"),
        P(("expert", "col"), None),
        P(("expert", "col"), None),
        P("expert", "row", "col"),
        P("expert", "row", "col"),
        P("expert", "col", "row"),
    )
    return jax.shard_map(
        on_device,
        mesh=mesh,
        in_specs=placed,
        out_specs=P(("expert", "col"), "row"),
        check_vma=False,
    )
```

```python
import jax
import jax.numpy as jnp
from jax import lax
from jax.experimental import pallas as pl
from jax.experimental.pallas import tpu as pltpu
from jax.sharding import PartitionSpec as P

MESH = pl.DeviceIdType.MESH
BF16 = jnp.bfloat16
F32 = jnp.float32

N_Y = 4
N_Z = 8
N_X = 4
T_DEV = 64
SUPER = N_Y * T_DEV
EXPERTS = 8
N_LOCAL = 4
PAIRS = 2 * SUPER
SHARD = PAIRS // N_X
HALF = SHARD // 2
META = 128
ORDER = (0, 1, 5, 7, 6, 3, 4, 2)
PLAN = (
    "a10 zp2 a20 y21",
    "zp3 y12 c0 a11",
    "zb1 a21 y22 zb3",
    "b0 zp4 y13 c1",
    "y14 a12 d0 a22",
    "b1 y23 e10 y24",
    "c2 zb2 e20 d1",
    "a13 a23 a14 b2",
    "c3 a24 a15 d2",
    "a25 b3 e11 c4",
    "g0 e21 c5 a16",
    "e12 d3 e22 b4",
    "a26 a17 b5 g2",
    "d4 e13 c6 e23",
    "g1 a27 d5 e14",
    "h0 g3 b6 e24",
    "c7 e15 h1 d6",
    "e25 h3 zr0 g4",
    "h2 b7 e16 e26",
    "g5 d7 h4 zr1",
    "g6 e17 e27 h5",
    "h6 zr2 g7 h7",
    "zr3",
)
SUMS = 6
DEEP = 5


def dot(a, b):
    return jnp.dot(a, b, preferred_element_type=F32)


def dot_nt(a, b):
    return lax.dot_general(a, b, (((1,), (1,)), ((), ())), preferred_element_type=F32)


def same(n):
    one = lax.broadcasted_iota(jnp.int32, (n, n), 0) == lax.broadcasted_iota(jnp.int32, (n, n), 1)
    return one.astype(F32).astype(BF16)


def kernel(
    tok_hbm, ids_hbm, rw_hbm, wg_hbm, wu_hbm, wd_hbm, out_ref,
    ids_ref, rw_ref, wg, wu, wd, xbuf, dense, gubuf, r1, r2, hbuf, spread, yb, ry1, ry2, zp, zs, zr,
    in_sem, w_sem, ws_s, ws_r, zb_s, zb_r, ya_s, ya1_r, ya2_r, gz_s, gz_r, x_s, x1_r, x2_r, h_s, h1_r, h2_r,
    y_s, y1_r, y2_r, z_s, z_r,
):
    feat = tok_hbm.shape[1]
    hid = wg.shape[2]
    e = lax.axis_index("expert")
    x = lax.axis_index("row")
    c = lax.axis_index("col")
    z = c // N_Y
    y = c % N_Y
    xp, xm, xo = (x + 1) % N_X, (x + 3) % N_X, (x + 2) % N_X
    yp, ym, yo = (y + 1) % N_Y, (y + 3) % N_Y, (y + 2) % N_Y
    zup, zdn = (z + 1) % N_Z, (z + N_Z - 1) % N_Z
    partner = (1 - e, x, c)
    dev_xp, dev_xm = (e, xp, c), (e, xm, c)
    dev_yp, dev_ym = (e, x, z * N_Y + yp), (e, x, z * N_Y + ym)
    dev_zu, dev_zd = (e, x, zup * N_Y + y), (e, x, zdn * N_Y + y)

    barrier = pltpu.get_barrier_semaphore()
    for dev in (partner, dev_xp, dev_xm, dev_yp, dev_ym, dev_zu, dev_zd):
        pl.semaphore_signal(barrier, inc=1, device_id=dev, device_id_type=MESH)

    own = xbuf.at[z, y]
    inputs = (
        pltpu.make_async_copy(ids_hbm, ids_ref, in_sem.at[0]),
        pltpu.make_async_copy(rw_hbm, rw_ref, in_sem.at[1]),
        pltpu.make_async_copy(tok_hbm, own.at[:, pl.ds(0, feat)], in_sem.at[2]),
    )
    for copy in inputs:
        copy.start()
    mine = pl.ds(e * N_LOCAL, N_LOCAL)
    theirs = pl.ds((1 - e) * N_LOCAL, N_LOCAL)
    loads = []
    for n, (src, dst) in enumerate(((wg_hbm, wg), (wu_hbm, wu), (wd_hbm, wd))):
        loads.append(pltpu.make_async_copy(src, dst.at[mine], w_sem.at[n]))
        loads[-1].start()

    def send(src, dst, ssem, rsem, dev):
        return pltpu.make_async_remote_copy(
            src_ref=src, dst_ref=dst, send_sem=ssem, recv_sem=rsem, device_id=dev,
            device_id_type=MESH,
        )

    def landed(dst, rsem):
        send(dst, dst, rsem, rsem, partner).wait_recv()

    def left(src, ssem):
        send(src, src, ssem, ssem, partner).wait_send()

    def place(j):
        off = (j // 2) * (1 - j % 2) - ((j + 1) // 2) * (j % 2)
        return (z + off + N_Z) % N_Z

    def chunk(i):
        return place(ORDER[i])

    inputs[0].wait()
    inputs[1].wait()
    line = lax.broadcasted_iota(jnp.int32, (META, T_DEV), 0)
    lines = jnp.zeros((META, T_DEV), F32)
    for k in range(2):
        lines = jnp.where(line == k, ids_ref[k : k + 1].astype(F32), lines)
        rest = rw_ref[k : k + 1]
        for part in range(3):
            piece = rest.astype(BF16).astype(F32)
            lines = jnp.where(line == 2 + 3 * k + part, piece, lines)
            rest = rest - piece
    xbuf[z, y, :, feat : feat + META] = dot_nt(same(T_DEV), lines.astype(BF16)).astype(BF16)
    inputs[2].wait()

    pl.semaphore_wait(barrier, 7)

    half = T_DEV // 2
    low, high = pl.ds(0, half), pl.ds(half, half)

    def hop_gz(at):
        j, up = (0, at == 0) if at in (0, 7) else (at, at % 2 == 1)
        part = xbuf.at[place(j), y]
        to = j + 2 if j else (1 if up else 2)
        if j > 4:
            part, to = part.at[low if up else high], (7 if up else 8)
        return send(part, part, gz_s.at[at], gz_r.at[to], dev_zu if up else dev_zd)

    def stage_zp(k):
        j = 2 * k - 1
        block = xbuf.at[place(j), y]
        if j == 7:
            landed(block.at[low], gz_r.at[7])
            landed(block.at[high], gz_r.at[8])
            return
        landed(block, gz_r.at[j])
        hop_gz(j).start()
        landed(xbuf.at[place(j + 1), y], gz_r.at[j + 1])
        hop_gz(j + 1).start()

    def stage_y1(k):
        block = xbuf.at[chunk(k), y]
        send(block, block, ya_s.at[k], ya1_r.at[k], dev_yp).start()
        send(block, block, ya_s.at[k], ya1_r.at[k], dev_ym).start()

    def stage_y2(k):
        zc = chunk(k)
        landed(xbuf.at[zc, pl.ds(0, 2)], ya1_r.at[k])
        a, b = xbuf.at[zc, ym, low], xbuf.at[zc, yp, high]
        send(a, a, ya_s.at[k], ya2_r.at[k], dev_yp).start()
        send(b, b, ya_s.at[k], ya2_r.at[k], dev_ym).start()

    def hops_zb(n):
        zc = place((0, 2, 1)[n - 1])
        dev = dev_zu if n == 3 else dev_zd
        blocks = [xbuf.at[zc, b] for b in (yp, ym, yo)]
        return [send(block, block, zb_s.at[n - 1], zb_r.at[n - 1], dev) for block in blocks]

    def stage_zb(n):
        if n == 2:
            landed(xbuf.at[place(2), pl.ds(0, 3)], zb_r.at[0])
        for copy in hops_zb(n):
            copy.start()

    def to_partner(n):
        src, dst = ((wg_hbm, wg), (wu_hbm, wu), (wd_hbm, wd))[n]
        return send(src, dst.at[mine], ws_s.at[n], ws_r.at[n], partner)

    stage_y1(0)
    hop_gz(0).start()
    hop_gz(7).start()
    to_partner(0).start()
    to_partner(1).start()
    stage_y2(0)
    stage_zp(1)
    stage_y1(1)
    for copy in loads:
        copy.wait()

    def products(i, part):
        zc = chunk(i)
        for n in range(part * N_LOCAL, (part + 1) * N_LOCAL):
            v = (e * N_LOCAL + n) % EXPERTS if i == 0 else n
            rows = xbuf[zc, :, :, 0:feat].reshape(SUPER, feat)
            dense[v, :, 0:hid] = dot(rows, wg[v]).astype(BF16)
            dense[v, :, hid : 2 * hid] = dot(rows, wu[v]).astype(BF16)

    def choices(i, b):
        info = xbuf[chunk(i), b, :, feat : feat + META].astype(F32)
        wide = (T_DEV, hid)
        return jnp.broadcast_to(info[:, 0:1], wide), jnp.broadcast_to(info[:, 1:2], wide)

    def stage_a1(i):
        zc = chunk(i)
        if ORDER[i] in (3, 4):
            landed(xbuf.at[zc, pl.ds(0, 3)], zb_r.at[1 if ORDER[i] == 4 else 2])
        elif ORDER[i] != 2:
            landed(xbuf.at[zc, yo], ya2_r.at[i])
        products(i, 0)

    def stage_a2(i):
        par = i % SUMS
        if i == 0:
            landed(wg.at[theirs], ws_r.at[0])
            landed(wu.at[theirs], ws_r.at[1])
        products(i, 1)
        for b in range(N_Y):
            id0, id1 = choices(i, b)
            rows_in = slice(b * T_DEV, (b + 1) * T_DEV)
            rows_out = slice((b % 2) * T_DEV, (b % 2 + 1) * T_DEV)
            for n in range(0, 2 * hid, hid):
                first = second = jnp.zeros((T_DEV, hid), F32)
                for v in range(EXPERTS):
                    got = dense[v, rows_in, n : n + hid].astype(F32)
                    first = jnp.where(id0 == v, got, first)
                    second = jnp.where(id1 == v, got, second)
                gubuf[par, b // 2, rows_out, n : n + hid] = first.astype(BF16)
                gubuf[par, 2 + b // 2, rows_out, n : n + hid] = second.astype(BF16)
        g = gubuf.at[par]
        send(g.at[xo, top], r1.at[i, 0], x_s.at[i], x1_r.at[i], dev_xp).start()
        send(g.at[xo, bot], r1.at[i, 1], x_s.at[i], x1_r.at[i], dev_xm).start()
        if i == 0:
            to_partner(2).start()

    top, bot = pl.ds(0, HALF), pl.ds(HALF, HALF)

    def stage_c(i):
        par = i % SUMS
        g = gubuf.at[par]
        landed(r1.at[i], x1_r.at[i])
        gubuf[par, xp, top] = (
            gubuf[par, xp, top].astype(F32) + r1[i, 0].astype(F32)
        ).astype(BF16)
        send(g.at[xp], r2.at[i, 0], x_s.at[i], x2_r.at[i], dev_xp).start()
        gubuf[par, xm, bot] = (
            gubuf[par, xm, bot].astype(F32) + r1[i, 1].astype(F32)
        ).astype(BF16)
        send(g.at[xm], r2.at[i, 1], x_s.at[i], x2_r.at[i], dev_xm).start()

    def stage_b(i):
        par = i % SUMS
        landed(r2.at[i], x2_r.at[i])
        total = gubuf[par, x].astype(F32) + r2[i, 0].astype(F32) + r2[i, 1].astype(F32)
        gate, up = total[:, 0:hid], total[:, hid : 2 * hid]
        info = xbuf[chunk(i), pl.ds((x % 2) * 2, 2), :, feat : feat + META]
        info = info.reshape(SHARD, META).astype(F32)
        w0 = info[:, 2:3] + info[:, 3:4] + info[:, 4:5]
        w1 = info[:, 5:6] + info[:, 6:7] + info[:, 7:8]
        weight = jnp.where(x // 2 == 1, w1, w0)
        hbuf[i, x] = (gate / (1.0 + jnp.exp(-gate)) * up * weight).astype(BF16)
        block = hbuf.at[i, x]
        send(block, block, h_s.at[i], h1_r.at[i], dev_xp).start()
        send(block, block, h_s.at[i], h1_r.at[i], dev_xm).start()
        left(gubuf.at[par, pl.ds(0, 3)], x_s.at[i])

    def stage_d(i):
        landed(hbuf.at[i, pl.ds(0, 2)], h1_r.at[i])
        a, b = hbuf.at[i, xm, top], hbuf.at[i, xp, bot]
        send(a, a, h_s.at[i], h2_r.at[i], dev_xp).start()
        send(b, b, h_s.at[i], h2_r.at[i], dev_xm).start()

    def mixed(i, columns):
        rows = wd.reshape(EXPERTS * hid, feat)
        for n in columns:
            part = dot(spread[...], rows[:, n : n + 256])
            yb[i % DEEP, :, :, n : n + 256] = part.astype(BF16).reshape(N_Y, T_DEV, 256)

    def stage_e1(i):
        landed(hbuf.at[i, xo], h2_r.at[i])
        if i == 0:
            landed(wd.at[theirs], ws_r.at[2])
        for b in range(N_Y):
            id0, id1 = choices(i, b)
            rows = slice((b % 2) * T_DEV, (b % 2 + 1) * T_DEV)
            first = hbuf[i, b // 2, rows].astype(F32)
            second = hbuf[i, 2 + b // 2, rows].astype(F32)
            for v in range(EXPERTS):
                here = jnp.where(id0 == v, first, jnp.where(id1 == v, second, 0.0))
                spread[b * T_DEV : (b + 1) * T_DEV, v * hid : (v + 1) * hid] = here.astype(BF16)
        mixed(i, range(0, feat // 2, 256))

    def stage_e2(i):
        block = yb.at[i % DEEP]
        mixed(i, range(feat // 2, feat, 256))
        send(block.at[yo, low], ry1.at[i, 0], y_s.at[i], y1_r.at[i], dev_yp).start()
        send(block.at[yo, high], ry1.at[i, 1], y_s.at[i], y1_r.at[i], dev_ym).start()
        send(block.at[yp, high], ry2.at[i, 0, high], y_s.at[i], y2_r.at[i], dev_yp).start()
        send(block.at[ym, low], ry2.at[i, 1, low], y_s.at[i], y2_r.at[i], dev_ym).start()

    def stage_g(i):
        par = i % DEEP
        block = yb.at[par]
        landed(ry1.at[i], y1_r.at[i])
        yb[par, yp, low] = (yb[par, yp, low].astype(F32) + ry1[i, 0].astype(F32)).astype(BF16)
        send(block.at[yp, low], ry2.at[i, 0, low], y_s.at[i], y2_r.at[i], dev_yp).start()
        yb[par, ym, high] = (yb[par, ym, high].astype(F32) + ry1[i, 1].astype(F32)).astype(BF16)
        send(block.at[ym, high], ry2.at[i, 1, high], y_s.at[i], y2_r.at[i], dev_ym).start()

    def stage_h(i):
        par = i % DEEP
        landed(ry2.at[i], y2_r.at[i])
        zp[chunk(i)] = yb[par, y].astype(F32) + ry2[i, 0].astype(F32) + ry2[i, 1].astype(F32)
        left(yb.at[par, pl.ds(0, 3)], y_s.at[i])

    def hop_z(k, way):
        dev = dev_zd if way == 0 else dev_zu
        part = zs.at[way, k]
        into = zr.at[way, k]
        if k == 0:
            rows = low if way == 0 else high
            part, into = part.at[rows], into.at[rows]
        return send(part, into, z_s.at[way, k], z_r.at[way, k], dev)

    def stage_zr(k):
        for way in range(2):
            far = 4 - k
            dest = (z + (N_Z - far if way == 0 else far)) % N_Z
            rows, other = (low, high) if way == 0 else (high, low)
            if k == 0:
                zs[way, k, rows] = zp[dest, rows].astype(BF16)
            elif k == 1:
                landed(zr.at[way, 0, rows], z_r.at[way, 0])
                zs[way, k, other] = zp[dest, other].astype(BF16)
                zs[way, k, rows] = (zp[dest, rows] + zr[way, 0, rows].astype(F32)).astype(BF16)
            else:
                landed(zr.at[way, k - 1], z_r.at[way, k - 1])
                zs[way, k] = (zp[dest] + zr[way, k - 1].astype(F32)).astype(BF16)
            hop_z(k, way).start()

    stages = dict(
        y1=stage_y1, y2=stage_y2, a1=stage_a1, a2=stage_a2, b=stage_b, c=stage_c,
        d=stage_d, e1=stage_e1, e2=stage_e2, g=stage_g, h=stage_h, zp=stage_zp, zr=stage_zr, zb=stage_zb,
    )
    for line_of_plan in PLAN:
        for step in line_of_plan.split():
            stages[step[:-1]](int(step[-1]))

    landed(zr.at[0, 3], z_r.at[0, 3])
    landed(zr.at[1, 3], z_r.at[1, 3])
    out_ref[...] = (zp[z] + zr[0, 3].astype(F32) + zr[1, 3].astype(F32)).astype(BF16)

    for k in range(4):
        for way in range(2):
            hop_z(k, way).wait_send()
    for at in range(8):
        hop_gz(at).wait_send()
    for n in range(3):
        to_partner(n).wait_send()
        for copy in hops_zb(n + 1):
            copy.wait_send()
    for k in range(N_Z):
        if ORDER[k] not in (2, 3, 4):
            left(xbuf.at[z, pl.ds(0, 3)], ya_s.at[k])
        left(hbuf.at[k, pl.ds(0, 3)], h_s.at[k])


def on_device(tokens, expert_ids, route_weight, gate_w, up_w, down_w):
    t_dev, feat = tokens.shape
    hid = gate_w.shape[2]
    hbm = pl.BlockSpec(memory_space=pl.ANY)
    dma = pltpu.SemaphoreType.DMA
    eight = dma((8,))
    return pl.pallas_call(
        kernel,
        out_shape=jax.ShapeDtypeStruct((t_dev, feat), BF16),
        in_specs=[hbm] * 6,
        out_specs=pl.BlockSpec(memory_space=pltpu.VMEM),
        scratch_shapes=[
            pltpu.VMEM((2, t_dev), jnp.int32),
            pltpu.VMEM((2, t_dev), F32),
            pltpu.VMEM((EXPERTS, feat, hid), BF16),
            pltpu.VMEM((EXPERTS, feat, hid), BF16),
            pltpu.VMEM((EXPERTS, hid, feat), BF16),
            pltpu.VMEM((N_Z, N_Y, T_DEV, feat + META), BF16),
            pltpu.VMEM((EXPERTS, SUPER, 2 * hid), BF16),
            pltpu.VMEM((SUMS, N_X, SHARD, 2 * hid), BF16),
            pltpu.VMEM((N_Z, 2, HALF, 2 * hid), BF16),
            pltpu.VMEM((N_Z, 2, SHARD, 2 * hid), BF16),
            pltpu.VMEM((N_Z, N_X, SHARD, hid), BF16),
            pltpu.VMEM((SUPER, EXPERTS * hid), BF16),
            pltpu.VMEM((DEEP, N_Y, T_DEV, feat), BF16),
            pltpu.VMEM((N_Z, 2, T_DEV // 2, feat), BF16),
            pltpu.VMEM((N_Z, 2, T_DEV, feat), BF16),
            pltpu.VMEM((N_Z, T_DEV, feat), F32),
            pltpu.VMEM((2, 4, T_DEV, feat), BF16),
            pltpu.VMEM((2, 4, T_DEV, feat), BF16),
            dma((3,)), dma((3,)), dma((3,)), dma((3,)), dma((3,)), dma((3,)),
            eight, eight, eight,
            eight, dma((9,)),
            eight, eight, eight,
            eight, eight, eight,
            eight, eight, eight,
            dma((2, 4)), dma((2, 4)),
        ],
        compiler_params=pltpu.CompilerParams(
            collective_id=0, has_side_effects=True, vmem_limit_bytes=58 * 1024 * 1024
        ),
        cost_estimate=pl.CostEstimate(
            flops=14_000_000_000, bytes_accessed=8_000_000, transcendentals=2_000_000
        ),
        name="moe_layer",
    )(tokens, expert_ids.T, route_weight.T, gate_w, up_w, down_w)


def solution(mesh):
    placed = (
        P(("expert", "col"), "row"),
        P(("expert", "col"), None),
        P(("expert", "col"), None),
        P("expert", "row", "col"),
        P("expert", "row", "col"),
        P("expert", "col", "row"),
    )
    return jax.shard_map(
        on_device,
        mesh=mesh,
        in_specs=placed,
        out_specs=P(("expert", "col"), "row"),
        check_vma=False,
    )
```

```python
import jax
import jax.numpy as jnp
from jax import lax
from jax.experimental import pallas as pl
from jax.experimental.pallas import tpu as pltpu
from jax.sharding import PartitionSpec as P

MESH = pl.DeviceIdType.MESH
BF16 = jnp.bfloat16
F32 = jnp.float32

N_Y = 4
N_Z = 8
N_X = 4
T_DEV = 64
SUPER = N_Y * T_DEV
EXPERTS = 8
N_LOCAL = 4
PAIRS = 2 * SUPER
SHARD = PAIRS // N_X
HALF = SHARD // 2
META = 128
ORDER = (0, 1, 5, 7, 6, 3, 4, 2)
PLAN = (
    "zp2 a10 y21 a20",
    "zp3 y12 a11 y14",
    "c0 zb1 a21 zb3",
    "y22 zp4 y13 b0",
    "c1 a12 d0 a22",
    "y23 b1 y24 zb2",
    "e10 c2 a13 a23",
    "e20 d1 b2 a14",
    "c3 a24 d2 a15",
    "a25 b3 g0 c4",
    "e11 e21 e12 e22",
    "c5 d3 a16 h0",
    "b4 g1 a26 a17",
    "b5 e13 d4 e23",
    "c6 a27 g2 e14",
    "e24 g3 d5 b6",
    "h1 c7 g4 e15",
    "d6 e25 h3 h2",
    "zr0 b7 e16 e26",
    "h4 zr1 d7 g5",
    "g6 e17 e27 h5",
    "h6 zr2 g7 h7",
    "zr3",
)
SUMS = 6
DEEP = 5


def dot(a, b):
    return jnp.dot(a, b, preferred_element_type=F32)


def dot_nt(a, b):
    return lax.dot_general(a, b, (((1,), (1,)), ((), ())), preferred_element_type=F32)


def same(n):
    one = lax.broadcasted_iota(jnp.int32, (n, n), 0) == lax.broadcasted_iota(jnp.int32, (n, n), 1)
    return one.astype(F32).astype(BF16)


def kernel(
    tok_hbm, ids_hbm, rw_hbm, wg_hbm, wu_hbm, wd_hbm, out_ref,
    ids_ref, rw_ref, wg, wu, wd, xbuf, dense, gubuf, r1, r2, hbuf, spread, yb, ry1, ry2, zp, zs, zr,
    in_sem, w_sem, ws_s, ws_r, zb_s, zb_r, ya_s, ya1_r, ya2_r, gz_s, gz_r, x_s, x1_r, x2_r, h_s, h1_r, h2_r,
    y_s, y1_r, y2_r, z_s, z_r, turn,
):
    feat = tok_hbm.shape[1]
    hid = wg.shape[2]
    e = lax.axis_index("expert")
    x = lax.axis_index("row")
    c = lax.axis_index("col")
    z = c // N_Y
    y = c % N_Y
    xp, xm, xo = (x + 1) % N_X, (x + 3) % N_X, (x + 2) % N_X
    yp, ym, yo = (y + 1) % N_Y, (y + 3) % N_Y, (y + 2) % N_Y
    zup, zdn = (z + 1) % N_Z, (z + N_Z - 1) % N_Z
    partner = (1 - e, x, c)
    dev_xp, dev_xm = (e, xp, c), (e, xm, c)
    dev_yp, dev_ym = (e, x, z * N_Y + yp), (e, x, z * N_Y + ym)
    dev_zu, dev_zd = (e, x, zup * N_Y + y), (e, x, zdn * N_Y + y)

    barrier = pltpu.get_barrier_semaphore()
    for dev in (partner, dev_xp, dev_xm, dev_yp, dev_ym, dev_zu, dev_zd):
        pl.semaphore_signal(barrier, inc=1, device_id=dev, device_id_type=MESH)

    own = xbuf.at[z, y]
    inputs = (
        pltpu.make_async_copy(ids_hbm, ids_ref, in_sem.at[0]),
        pltpu.make_async_copy(rw_hbm, rw_ref, in_sem.at[1]),
        pltpu.make_async_copy(tok_hbm, own.at[:, pl.ds(0, feat)], in_sem.at[2]),
    )
    for copy in inputs:
        copy.start()
    mine = pl.ds(e * N_LOCAL, N_LOCAL)
    theirs = pl.ds((1 - e) * N_LOCAL, N_LOCAL)
    loads = []
    for n, (src, dst) in enumerate(((wg_hbm, wg), (wu_hbm, wu), (wd_hbm, wd))):
        loads.append(pltpu.make_async_copy(src, dst.at[mine], w_sem.at[n]))
        loads[-1].start()

    def send(src, dst, ssem, rsem, dev):
        return pltpu.make_async_remote_copy(
            src_ref=src, dst_ref=dst, send_sem=ssem, recv_sem=rsem, device_id=dev,
            device_id_type=MESH,
        )

    def landed(dst, rsem):
        send(dst, dst, rsem, rsem, partner).wait_recv()

    def left(src, ssem):
        send(src, src, ssem, ssem, partner).wait_send()

    def place(j):
        off = (j // 2) * (1 - j % 2) - ((j + 1) // 2) * (j % 2)
        return (z + off + N_Z) % N_Z

    def chunk(i):
        return place(ORDER[i])

    inputs[0].wait()
    inputs[1].wait()
    line = lax.broadcasted_iota(jnp.int32, (META, T_DEV), 0)
    lines = jnp.zeros((META, T_DEV), F32)
    for k in range(2):
        lines = jnp.where(line == k, ids_ref[k : k + 1].astype(F32), lines)
        rest = rw_ref[k : k + 1]
        for part in range(3):
            piece = rest.astype(BF16).astype(F32)
            lines = jnp.where(line == 2 + 3 * k + part, piece, lines)
            rest = rest - piece
    xbuf[z, y, :, feat : feat + META] = dot_nt(same(T_DEV), lines.astype(BF16)).astype(BF16)
    inputs[2].wait()

    pl.semaphore_wait(barrier, 7)

    half = T_DEV // 2
    low, high = pl.ds(0, half), pl.ds(half, half)

    def hop_gz(at):
        j, up = (0, at == 0) if at in (0, 7) else (at, at % 2 == 1)
        part = xbuf.at[place(j), y]
        to = j + 2 if j else (1 if up else 2)
        if j > 4:
            part, to = part.at[low if up else high], (7 if up else 8)
        return send(part, part, gz_s.at[at], gz_r.at[to], dev_zu if up else dev_zd)

    def stage_zp(k):
        j = 2 * k - 1
        block = xbuf.at[place(j), y]
        if j == 7:
            landed(block.at[low], gz_r.at[7])
            landed(block.at[high], gz_r.at[8])
            return
        landed(block, gz_r.at[j])
        hop_gz(j).start()
        landed(xbuf.at[place(j + 1), y], gz_r.at[j + 1])
        hop_gz(j + 1).start()

    def stage_y1(k):
        block = xbuf.at[chunk(k), y]
        send(block, block, ya_s.at[k], ya1_r.at[k], dev_yp).start()
        send(block, block, ya_s.at[k], ya1_r.at[k], dev_ym).start()

    def stage_y2(k):
        zc = chunk(k)
        landed(xbuf.at[zc, pl.ds(0, 2)], ya1_r.at[k])
        a, b = xbuf.at[zc, ym, low], xbuf.at[zc, yp, high]
        send(a, a, ya_s.at[k], ya2_r.at[k], dev_yp).start()
        send(b, b, ya_s.at[k], ya2_r.at[k], dev_ym).start()

    def hops_zb(n):
        zc = place((0, 2, 1)[n - 1])
        dev = dev_zu if n == 3 else dev_zd
        blocks = [xbuf.at[zc, b] for b in (yp, ym, yo)]
        return [send(block, block, zb_s.at[n - 1], zb_r.at[n - 1], dev) for block in blocks]

    def stage_zb(n):
        if n == 2:
            landed(xbuf.at[place(2), pl.ds(0, 3)], zb_r.at[0])
        for copy in hops_zb(n):
            copy.start()

    def to_partner(n):
        src, dst = ((wg_hbm, wg), (wu_hbm, wu), (wd_hbm, wd))[n]
        return send(src, dst.at[mine], ws_s.at[n], ws_r.at[n], partner)

    to_partner(0).start()
    to_partner(1).start()

    @pl.when(e == 1)
    def _():
        pl.semaphore_wait(turn, 1)

    stage_y1(0)
    hop_gz(0).start()
    hop_gz(7).start()
    stage_y2(0)

    @pl.when(e == 0)
    def _():
        pl.semaphore_signal(turn, inc=1, device_id=partner, device_id_type=MESH)

    stage_zp(1)
    stage_y1(1)
    for copy in loads:
        copy.wait()

    def products(i, part):
        zc = chunk(i)
        for n in range(part * N_LOCAL, (part + 1) * N_LOCAL):
            v = (e * N_LOCAL + n) % EXPERTS if i == 0 else n
            rows = xbuf[zc, :, :, 0:feat].reshape(SUPER, feat)
            dense[v, :, 0:hid] = dot(rows, wg[v]).astype(BF16)
            dense[v, :, hid : 2 * hid] = dot(rows, wu[v]).astype(BF16)

    def choices(i, b):
        info = xbuf[chunk(i), b, :, feat : feat + META].astype(F32)
        wide = (T_DEV, hid)
        return jnp.broadcast_to(info[:, 0:1], wide), jnp.broadcast_to(info[:, 1:2], wide)

    def stage_a1(i):
        zc = chunk(i)
        if ORDER[i] in (3, 4):
            landed(xbuf.at[zc, pl.ds(0, 3)], zb_r.at[1 if ORDER[i] == 4 else 2])
        elif ORDER[i] != 2:
            landed(xbuf.at[zc, yo], ya2_r.at[i])
        products(i, 0)

    def stage_a2(i):
        par = i % SUMS
        if i == 0:
            landed(wg.at[theirs], ws_r.at[0])
            landed(wu.at[theirs], ws_r.at[1])
        products(i, 1)
        for b in range(N_Y):
            id0, id1 = choices(i, b)
            rows_in = slice(b * T_DEV, (b + 1) * T_DEV)
            rows_out = slice((b % 2) * T_DEV, (b % 2 + 1) * T_DEV)
            for n in range(0, 2 * hid, hid):
                first = second = jnp.zeros((T_DEV, hid), F32)
                for v in range(EXPERTS):
                    got = dense[v, rows_in, n : n + hid].astype(F32)
                    first = jnp.where(id0 == v, got, first)
                    second = jnp.where(id1 == v, got, second)
                gubuf[par, b // 2, rows_out, n : n + hid] = first.astype(BF16)
                gubuf[par, 2 + b // 2, rows_out, n : n + hid] = second.astype(BF16)
        g = gubuf.at[par]
        send(g.at[xo, top], r1.at[i, 0], x_s.at[i], x1_r.at[i], dev_xp).start()
        send(g.at[xo, bot], r1.at[i, 1], x_s.at[i], x1_r.at[i], dev_xm).start()
        if i == 0:
            to_partner(2).start()

    top, bot = pl.ds(0, HALF), pl.ds(HALF, HALF)

    def stage_c(i):
        par = i % SUMS
        g = gubuf.at[par]
        landed(r1.at[i], x1_r.at[i])
        gubuf[par, xp, top] = (
            gubuf[par, xp, top].astype(F32) + r1[i, 0].astype(F32)
        ).astype(BF16)
        send(g.at[xp], r2.at[i, 0], x_s.at[i], x2_r.at[i], dev_xp).start()
        gubuf[par, xm, bot] = (
            gubuf[par, xm, bot].astype(F32) + r1[i, 1].astype(F32)
        ).astype(BF16)
        send(g.at[xm], r2.at[i, 1], x_s.at[i], x2_r.at[i], dev_xm).start()

    def stage_b(i):
        par = i % SUMS
        landed(r2.at[i], x2_r.at[i])
        total = gubuf[par, x].astype(F32) + r2[i, 0].astype(F32) + r2[i, 1].astype(F32)
        gate, up = total[:, 0:hid], total[:, hid : 2 * hid]
        info = xbuf[chunk(i), pl.ds((x % 2) * 2, 2), :, feat : feat + META]
        info = info.reshape(SHARD, META).astype(F32)
        w0 = info[:, 2:3] + info[:, 3:4] + info[:, 4:5]
        w1 = info[:, 5:6] + info[:, 6:7] + info[:, 7:8]
        weight = jnp.where(x // 2 == 1, w1, w0)
        hbuf[i, x] = (gate / (1.0 + jnp.exp(-gate)) * up * weight).astype(BF16)
        block = hbuf.at[i, x]
        send(block, block, h_s.at[i], h1_r.at[i], dev_xp).start()
        send(block, block, h_s.at[i], h1_r.at[i], dev_xm).start()
        left(gubuf.at[par, pl.ds(0, 3)], x_s.at[i])

    def stage_d(i):
        landed(hbuf.at[i, pl.ds(0, 2)], h1_r.at[i])
        a, b = hbuf.at[i, xm, top], hbuf.at[i, xp, bot]
        send(a, a, h_s.at[i], h2_r.at[i], dev_xp).start()
        send(b, b, h_s.at[i], h2_r.at[i], dev_xm).start()

    def mixed(i, columns):
        rows = wd.reshape(EXPERTS * hid, feat)
        for n in columns:
            part = dot(spread[...], rows[:, n : n + 256])
            yb[i % DEEP, :, :, n : n + 256] = part.astype(BF16).reshape(N_Y, T_DEV, 256)

    def stage_e1(i):
        landed(hbuf.at[i, xo], h2_r.at[i])
        if i == 0:
            landed(wd.at[theirs], ws_r.at[2])
        for b in range(N_Y):
            id0, id1 = choices(i, b)
            rows = slice((b % 2) * T_DEV, (b % 2 + 1) * T_DEV)
            first = hbuf[i, b // 2, rows].astype(F32)
            second = hbuf[i, 2 + b // 2, rows].astype(F32)
            for v in range(EXPERTS):
                here = jnp.where(id0 == v, first, jnp.where(id1 == v, second, 0.0))
                spread[b * T_DEV : (b + 1) * T_DEV, v * hid : (v + 1) * hid] = here.astype(BF16)
        mixed(i, range(0, feat // 2, 256))

    def stage_e2(i):
        block = yb.at[i % DEEP]
        mixed(i, range(feat // 2, feat, 256))
        send(block.at[yo, low], ry1.at[i, 0], y_s.at[i], y1_r.at[i], dev_yp).start()
        send(block.at[yo, high], ry1.at[i, 1], y_s.at[i], y1_r.at[i], dev_ym).start()
        send(block.at[yp, high], ry2.at[i, 0, high], y_s.at[i], y2_r.at[i], dev_yp).start()
        send(block.at[ym, low], ry2.at[i, 1, low], y_s.at[i], y2_r.at[i], dev_ym).start()

    def stage_g(i):
        par = i % DEEP
        block = yb.at[par]
        landed(ry1.at[i], y1_r.at[i])
        yb[par, yp, low] = (yb[par, yp, low].astype(F32) + ry1[i, 0].astype(F32)).astype(BF16)
        send(block.at[yp, low], ry2.at[i, 0, low], y_s.at[i], y2_r.at[i], dev_yp).start()
        yb[par, ym, high] = (yb[par, ym, high].astype(F32) + ry1[i, 1].astype(F32)).astype(BF16)
        send(block.at[ym, high], ry2.at[i, 1, high], y_s.at[i], y2_r.at[i], dev_ym).start()

    def stage_h(i):
        par = i % DEEP
        landed(ry2.at[i], y2_r.at[i])
        zp[chunk(i)] = yb[par, y].astype(F32) + ry2[i, 0].astype(F32) + ry2[i, 1].astype(F32)
        left(yb.at[par, pl.ds(0, 3)], y_s.at[i])

    def hop_z(k, way):
        dev = dev_zd if way == 0 else dev_zu
        part = zs.at[way, k]
        into = zr.at[way, k]
        if k == 0:
            rows = low if way == 0 else high
            part, into = part.at[rows], into.at[rows]
        return send(part, into, z_s.at[way, k], z_r.at[way, k], dev)

    def stage_zr(k):
        for way in range(2):
            far = 4 - k
            dest = (z + (N_Z - far if way == 0 else far)) % N_Z
            rows, other = (low, high) if way == 0 else (high, low)
            if k == 0:
                zs[way, k, rows] = zp[dest, rows].astype(BF16)
            elif k == 1:
                landed(zr.at[way, 0, rows], z_r.at[way, 0])
                zs[way, k, other] = zp[dest, other].astype(BF16)
                zs[way, k, rows] = (zp[dest, rows] + zr[way, 0, rows].astype(F32)).astype(BF16)
            else:
                landed(zr.at[way, k - 1], z_r.at[way, k - 1])
                zs[way, k] = (zp[dest] + zr[way, k - 1].astype(F32)).astype(BF16)
            hop_z(k, way).start()

    stages = dict(
        y1=stage_y1, y2=stage_y2, a1=stage_a1, a2=stage_a2, b=stage_b, c=stage_c,
        d=stage_d, e1=stage_e1, e2=stage_e2, g=stage_g, h=stage_h, zp=stage_zp, zr=stage_zr, zb=stage_zb,
    )
    for line_of_plan in PLAN:
        for step in line_of_plan.split():
            stages[step[:-1]](int(step[-1]))

    landed(zr.at[0, 3], z_r.at[0, 3])
    landed(zr.at[1, 3], z_r.at[1, 3])
    out_ref[...] = (zp[z] + zr[0, 3].astype(F32) + zr[1, 3].astype(F32)).astype(BF16)

    for k in range(4):
        for way in range(2):
            hop_z(k, way).wait_send()
    for at in range(8):
        hop_gz(at).wait_send()
    for n in range(3):
        to_partner(n).wait_send()
        for copy in hops_zb(n + 1):
            copy.wait_send()
    for k in range(N_Z):
        if ORDER[k] not in (2, 3, 4):
            left(xbuf.at[z, pl.ds(0, 3)], ya_s.at[k])
        left(hbuf.at[k, pl.ds(0, 3)], h_s.at[k])


def on_device(tokens, expert_ids, route_weight, gate_w, up_w, down_w):
    t_dev, feat = tokens.shape
    hid = gate_w.shape[2]
    hbm = pl.BlockSpec(memory_space=pl.ANY)
    dma = pltpu.SemaphoreType.DMA
    eight = dma((8,))
    return pl.pallas_call(
        kernel,
        out_shape=jax.ShapeDtypeStruct((t_dev, feat), BF16),
        in_specs=[hbm] * 6,
        out_specs=pl.BlockSpec(memory_space=pltpu.VMEM),
        scratch_shapes=[
            pltpu.VMEM((2, t_dev), jnp.int32),
            pltpu.VMEM((2, t_dev), F32),
            pltpu.VMEM((EXPERTS, feat, hid), BF16),
            pltpu.VMEM((EXPERTS, feat, hid), BF16),
            pltpu.VMEM((EXPERTS, hid, feat), BF16),
            pltpu.VMEM((N_Z, N_Y, T_DEV, feat + META), BF16),
            pltpu.VMEM((EXPERTS, SUPER, 2 * hid), BF16),
            pltpu.VMEM((SUMS, N_X, SHARD, 2 * hid), BF16),
            pltpu.VMEM((N_Z, 2, HALF, 2 * hid), BF16),
            pltpu.VMEM((N_Z, 2, SHARD, 2 * hid), BF16),
            pltpu.VMEM((N_Z, N_X, SHARD, hid), BF16),
            pltpu.VMEM((SUPER, EXPERTS * hid), BF16),
            pltpu.VMEM((DEEP, N_Y, T_DEV, feat), BF16),
            pltpu.VMEM((N_Z, 2, T_DEV // 2, feat), BF16),
            pltpu.VMEM((N_Z, 2, T_DEV, feat), BF16),
            pltpu.VMEM((N_Z, T_DEV, feat), F32),
            pltpu.VMEM((2, 4, T_DEV, feat), BF16),
            pltpu.VMEM((2, 4, T_DEV, feat), BF16),
            dma((3,)), dma((3,)), dma((3,)), dma((3,)), dma((3,)), dma((3,)),
            eight, eight, eight,
            eight, dma((9,)),
            eight, eight, eight,
            eight, eight, eight,
            eight, eight, eight,
            dma((2, 4)), dma((2, 4)),
            pltpu.SemaphoreType.REGULAR,
        ],
        compiler_params=pltpu.CompilerParams(
            collective_id=0, has_side_effects=True, vmem_limit_bytes=58 * 1024 * 1024
        ),
        cost_estimate=pl.CostEstimate(
            flops=14_000_000_000, bytes_accessed=8_000_000, transcendentals=2_000_000
        ),
        name="moe_layer",
    )(tokens, expert_ids.T, route_weight.T, gate_w, up_w, down_w)


def solution(mesh):
    placed = (
        P(("expert", "col"), "row"),
        P(("expert", "col"), None),
        P(("expert", "col"), None),
        P("expert", "row", "col"),
        P("expert", "row", "col"),
        P("expert", "col", "row"),
    )
    return jax.shard_map(
        on_device,
        mesh=mesh,
        in_specs=placed,
        out_specs=P(("expert", "col"), "row"),
        check_vma=False,
    )
```
